256 devices in a mesh: batch: 64 (over y_hi, x, z), rep: 4 (over y_lo, core).
Axes of the slice: x: 4, y: 4 (y_hi: 2, y_lo: 2; y = y_hi * 2 + y_lo), z: 8, core: 2. Of those that a mesh axis runs over, the one named last changes fastest.
Arguments:
- query_hidden: bfloat16 [4, 8192, 4096], P('rep', 'batch'), may hold values from -2 to 2
- passage_hidden: bfloat16 [4, 8192, 4096], P('rep', 'batch'), may hold values from -2 to 2
- norm_gain: float32 [4096], replicated, may hold values from 0.1 to 1.9
- negatives: int32 [4, 8192, 3], P('rep', 'batch'), may hold values from 0 to 8191, as said below
Outputs:
- query_grad: float32 [4, 8192, 4096], P('rep', 'batch')
- passage_grad: float32 [4, 8192, 4096], P('rep', 'batch')
- query_loss: float32 [4, 8192], P('rep', 'batch')
- gain_grad: float32 [4096], replicated
The draws below stay inside these ranges and needn't reach their ends.
Inputs may be any that keep to these rules, and one draw needn't show every extreme that they name: `negatives`: entries name passages of the query's own group; passage j lies on device j // 128 of batch, at row j % 128. The 384 entries of one device name any one owner at most 14 times and name at most 7 different passages of it. In every draw one owner is named exactly 14 times, through exactly 7 different passages, by every device of the group.
All inputs are finite; a program needn't handle non-finite values.
Results may differ from the reference program's by a relative error of at most 0.0047.
Values may be sent and summed in bfloat16 or wider, within the bound.
A program may use at most 128 MiB of HBM per device.

```python
import math
import jax
import jax.numpy as jnp
from jax import lax

D = 4096
TOK_DEV = 128
NEG = 3
STOPS = 4
PAIRS = 8192
N_BATCH = 64
N_REP = 4


def unit_values(key, shape):
    key_normal = jax.random.fold_in(key, 0)
    normal_part = jnp.clip(jax.random.normal(key_normal, shape, jnp.float32), -4.0, 4.0)
    return normal_part


def passage_units(key):
    base_key = jax.random.fold_in(key, 11)
    key_column = jax.random.fold_in(base_key, 0)
    key_units = jax.random.fold_in(base_key, 1)
    key_topic = jax.random.fold_in(base_key, 3)
    column = jnp.exp(jax.random.uniform(key_column, (D,), jnp.float32, 0.0, math.log(10.0)))
    strong = (jax.random.permutation(key_topic, D) < 256).astype(jnp.float32)
    column = column * (1.0 + 7.0 * strong)
    units = unit_values(key_units, (N_REP, PAIRS, D))
    return (column, units)


def route_table(key):
    base_key = jax.random.fold_in(key, 5)
    key_hot, key_order, key_start, key_other = jax.random.split(base_key, 4)
    request_count = TOK_DEV * NEG
    unique_cap = (request_count + N_BATCH - 1) // N_BATCH + 1
    capacity = 2 * unique_cap
    hot_owner = jax.random.randint(key_hot, (N_REP, 1, 1), 0, N_BATCH)
    request_pos = jnp.arange(request_count, dtype=jnp.int32)[None, None, :]
    start_row = jax.random.randint(key_start, (N_REP, N_BATCH, 1), 0, TOK_DEV)
    other_row = jax.random.randint(key_other, (N_REP, N_BATCH, request_count), 0, TOK_DEV)
    is_hot = request_pos < capacity
    spread_owner = (hot_owner + 1 + (request_pos - capacity) % (N_BATCH - 1)) % N_BATCH
    owner_dev = jnp.where(is_hot, hot_owner, spread_owner)
    row_index = jnp.where(is_hot, (start_row + request_pos % unique_cap) % TOK_DEV, other_row)
    passage_index = (owner_dev * TOK_DEV + row_index).astype(jnp.int32)
    order_keys = jax.random.randint(key_order, (N_REP, N_BATCH, request_count), 0, 65536) * request_count + request_pos
    shuffle_order = jnp.argsort(order_keys, axis=-1, stable=True)
    shuffled = jnp.take_along_axis(passage_index, shuffle_order, axis=-1)
    return shuffled.reshape(N_REP, PAIRS, NEG).astype(jnp.int32)


def row_scales(key, shape):
    return jnp.exp(jax.random.uniform(key, shape, jnp.float32, math.log(0.0006), math.log(0.006)))


def draw_query_hidden(key, part):
    column, units = passage_units(key)
    picked = route_table(key)
    key = jax.random.fold_in(key, 3)
    key_noise, key_scale = jax.random.split(key)
    mixed = units + 2.86 * unit_values(key_noise, (N_REP, PAIRS, D))
    for neg_slot in range(NEG):
        mixed = mixed + 0.8 * jax.vmap(lambda unit_table, chosen: unit_table[chosen])(units, picked[:, :, neg_slot])
    mixed = jnp.clip(mixed / math.sqrt(1.0 + 0.64 * NEG + 2.86 * 2.86), -4.0, 4.0)
    return (mixed * column * row_scales(key_scale, (N_REP, PAIRS, 1))).astype(jnp.bfloat16)


def draw_passage_hidden(key, part):
    column, units = passage_units(key)
    units = jnp.clip(units, -4.0, 4.0)
    key = jax.random.fold_in(key, 4)
    return (units * column * row_scales(key, (N_REP, PAIRS, 1))).astype(jnp.bfloat16)


def draw_negatives(key, part):
    return route_table(key)


def setup_inputs(seed: int = 0) -> dict:
    splits = jax.random.split(jax.random.key(seed), 5)
    query_hidden = draw_query_hidden(jax.random.fold_in(splits[4], 71), 0)
    passage_hidden = draw_passage_hidden(jax.random.fold_in(splits[4], 71), 0)
    norm_gain = jnp.clip(1.0 + 0.18 * jax.random.normal(splits[2], (D,), jnp.float32), 0.1, 1.9)
    negatives = draw_negatives(jax.random.fold_in(splits[4], 71), 0)
    return dict(query_hidden=query_hidden, passage_hidden=passage_hidden, norm_gain=norm_gain, negatives=negatives)


TEMP = 0.05
EPS = 1e-06

def unit_rows(hidden, norm_gain):
    scaled = hidden.astype(jnp.float32) * norm_gain
    length = jnp.sqrt(lax.optimization_barrier(jnp.sum(scaled * scaled, axis=-1, keepdims=True)) + EPS)
    return (scaled / length, length)

def norm_back(grad_rows, direct, length, hidden, norm_gain):
    inner_prod = lax.optimization_barrier(jnp.sum(direct * grad_rows, axis=-1, keepdims=True))
    dscaled = (grad_rows - direct * inner_prod) / length
    return (dscaled * norm_gain, lax.optimization_barrier(jnp.sum(hidden.astype(jnp.float32) * dscaled, axis=0)))

def one_group(q_hidden, p_hidden, wanted, norm_gain):
    q_dir, q_len = unit_rows(q_hidden, norm_gain)
    p_dir, p_len = unit_rows(p_hidden, norm_gain)
    q_emb = q_dir.astype(jnp.bfloat16)
    p_emb = p_dir.astype(jnp.bfloat16)
    p_blocks = p_emb.reshape(N_BATCH, TOK_DEV, D)
    q_blocks = q_emb.reshape(N_BATCH, TOK_DEV, D)
    w_blocks = wanted.reshape(N_BATCH, TOK_DEV, NEG)
    offsets = jnp.arange(STOPS, dtype=jnp.int32)
    identity = jnp.eye(TOK_DEV, dtype=jnp.float32)
    first_stop = (offsets == 0).astype(jnp.float32)
    positions = jnp.arange(TOK_DEV * NEG, dtype=jnp.int32)

    def visit(p_grad, inputs):
        block_index, queries, picked = inputs
        owners = ((block_index - offsets) % N_BATCH).astype(jnp.int32)
        window = p_blocks[owners]
        query_f32 = queries.astype(jnp.float32)
        scores = jnp.einsum('td,sjd->tsj', query_f32, window.astype(jnp.float32)) / TEMP
        fetched = p_emb[picked]
        neg_scores = jnp.einsum('td,tkd->tk', query_f32, fetched.astype(jnp.float32)) / TEMP
        exp_window = jnp.exp(scores)
        exp_negative = jnp.exp(neg_scores)
        partition = lax.optimization_barrier(jnp.sum(exp_window, axis=(1, 2))) + lax.optimization_barrier(jnp.sum(exp_negative, axis=1))
        inverse = 1.0 / partition
        query_loss = jnp.log(partition) - jnp.diagonal(scores[:, 0, :])
        weight = (exp_window * inverse[:, None, None] - first_stop[None, :, None] * identity[:, None, :]).astype(jnp.bfloat16)
        neg_weight = (exp_negative * inverse[:, None]).astype(jnp.bfloat16)
        q_grad = (jnp.einsum('tsj,sjd->td', weight.astype(jnp.float32), window.astype(jnp.float32)) + jnp.einsum('tk,tkd->td', neg_weight.astype(jnp.float32), fetched.astype(jnp.float32))) / TEMP
        block_terms = jnp.einsum('tsj,td->sjd', weight.astype(jnp.float32), query_f32) / TEMP
        rounded_terms = lax.optimization_barrier(block_terms.astype(jnp.bfloat16)).astype(jnp.float32)
        kept_terms = jnp.where(first_stop[:, None, None] > 0, block_terms, rounded_terms)
        p_grad = p_grad.at[owners].add(kept_terms)
        neg_rows = (neg_weight.astype(jnp.float32)[:, :, None] * query_f32[:, None, :] / TEMP).reshape(TOK_DEV * NEG, D)
        flat_pick = picked.reshape(-1).astype(jnp.int32)
        same_index = (flat_pick[:, None] == flat_pick[None, :]).astype(jnp.float32)
        first_seen = jnp.argmax(same_index, axis=1).astype(jnp.int32)
        leader = (first_seen == positions).astype(jnp.float32)
        summed = jnp.dot(same_index, neg_rows, precision=lax.Precision.HIGHEST, preferred_element_type=jnp.float32)
        summed = lax.optimization_barrier(summed.astype(jnp.bfloat16)).astype(jnp.float32) * leader[:, None]
        flat_grad = p_grad.reshape(PAIRS, D).at[flat_pick].add(summed)
        return (flat_grad.reshape(N_BATCH, TOK_DEV, D), (q_grad, query_loss))
    start_grad = jnp.zeros((N_BATCH, TOK_DEV, D), jnp.float32)
    p_grad, (q_grads, losses) = lax.scan(visit, start_grad, (jnp.arange(N_BATCH, dtype=jnp.int32), q_blocks, w_blocks))
    query_grad, gain_query = norm_back(q_grads.reshape(PAIRS, D), q_dir, q_len, q_hidden, norm_gain)
    passage_grad, gain_passage = norm_back(p_grad.reshape(PAIRS, D), p_dir, p_len, p_hidden, norm_gain)
    return (query_grad, passage_grad, losses.reshape(PAIRS), gain_query + gain_passage)

def reference(query_hidden, passage_hidden, norm_gain, negatives):

    def per_group(group_args):
        return one_group(group_args[0], group_args[1], group_args[2], norm_gain)
    query_grad, passage_grad, query_loss, gain_parts = lax.map(per_group, (query_hidden, passage_hidden, negatives))
    return (query_grad, passage_grad, query_loss, lax.optimization_barrier(jnp.sum(gain_parts, axis=0)))
```

```python
import functools

import jax
import jax.numpy as jnp
from jax import lax
from jax.experimental import pallas as pl
from jax.experimental.pallas import tpu as pltpu
from jax.sharding import PartitionSpec as P

STOPS = 4
TEMP = 0.05
EPS = 1e-06
SLOTS = 8
MIB = 1 << 20


def from_behind(block, axis, distance):
    size = lax.axis_size(axis)
    route = [((i - distance) % size, i) for i in range(size)]
    return lax.ppermute(block, axis, route)


def norm_kernel(q_ref, p_ref, gain_ref, qe_ref, pe_ref, x_ref, qn_ref, pn_ref):
    gain = gain_ref[...]
    units = []
    for src, emb, norm in ((q_ref, qe_ref, qn_ref), (p_ref, pe_ref, pn_ref)):
        scaled = src[...].astype(jnp.float32) * gain
        length = jnp.sqrt(jnp.sum(scaled * scaled, axis=-1, keepdims=True) + EPS)
        unit = scaled * (1.0 / length)
        emb[...] = unit.astype(jnp.bfloat16)
        norm[...] = jnp.broadcast_to(length, norm.shape)
        units.append(unit)
    q_unit, p_unit = units
    low = lax.broadcasted_iota(jnp.int32, (q_ref.shape[0], 128), 1) < 64
    for tile in range(q_ref.shape[1] // 128):
        q_tile = q_unit[:, tile * 128 : (tile + 1) * 128]
        p_tile = p_unit[:, tile * 128 : (tile + 1) * 128]
        x_ref[2 * tile] = jnp.where(low, q_tile, pltpu.roll(p_tile, 64, 1)).astype(jnp.bfloat16)
        x_ref[2 * tile + 1] = jnp.where(low, pltpu.roll(q_tile, 64, 1), p_tile).astype(jnp.bfloat16)


def normalize(q_hidden, p_hidden, gain):
    rows, width = q_hidden.shape
    tiles = width // 64
    step = 32
    row_block = pl.BlockSpec((step, width), lambda i: (i, 0))
    norm_block = pl.BlockSpec((step, 128), lambda i: (i, 0))
    return pl.pallas_call(
        norm_kernel,
        grid=(rows // step,),
        in_specs=[row_block, row_block, pl.BlockSpec((1, width), lambda i: (0, 0))],
        out_specs=[
            row_block,
            row_block,
            pl.BlockSpec((tiles, step, 128), lambda i: (0, i, 0)),
            norm_block,
            norm_block,
        ],
        out_shape=[
            jax.ShapeDtypeStruct((rows, width), jnp.bfloat16),
            jax.ShapeDtypeStruct((rows, width), jnp.bfloat16),
            jax.ShapeDtypeStruct((tiles, rows, 128), jnp.bfloat16),
            jax.ShapeDtypeStruct((rows, 128), jnp.float32),
            jax.ShapeDtypeStruct((rows, 128), jnp.float32),
        ],
        compiler_params=pltpu.CompilerParams(vmem_limit_bytes=32 * MIB),
        cost_estimate=pl.CostEstimate(flops=10 * rows * width, bytes_accessed=10 * rows * width, transcendentals=0),
        name="normalize",
    )(q_hidden, p_hidden, gain.reshape(1, width))


def neg_forward_kernel(half, hot_ref, w_ref, slot_ref, t_ref, table_ref, scratch):
    step = pl.program_id(0)

    @pl.when(step < half)
    def _():
        picked = []
        for part in range(2):
            rows = jnp.dot(hot_ref[part], w_ref[2 * step + part], preferred_element_type=jnp.float32)
            picked.append(rows.reshape(-1, SLOTS, 128))
        both = jnp.concatenate(picked, axis=1).astype(jnp.bfloat16)
        scratch[:, pl.ds(pl.multiple_of(step * 16, 16), 16), :] = both

    @pl.when(step >= half)
    def _():
        pair = step - half
        for part in range(2):
            device = 2 * pair + part
            table = scratch[device]
            table_ref[part] = table
            mine = w_ref[device].astype(jnp.float32)
            lane = lax.broadcasted_iota(jnp.int32, mine.shape, 1)
            query = jnp.where(lane < 64, 0.0, pltpu.roll(mine, 64, 1)).astype(jnp.bfloat16)
            scores = lax.dot_general(
                table, query, (((1,), (1,)), ((), ())), preferred_element_type=jnp.float32
            )
            place = lax.broadcasted_iota(jnp.int32, scores.shape, 0)
            for k in range(t_ref.shape[1]):
                hit = place == slot_ref[part, k : k + 1, :]
                t_ref[part, k : k + 1, :] = jnp.sum(jnp.where(hit, scores, 0.0), axis=0, keepdims=True)


def neg_forward(hot, w, slots):
    peers, places, rows = hot.shape
    neg = slots.shape[1]
    half = peers // 2
    late = lambda i: (jnp.maximum(i - half, 0), 0, 0)
    return pl.pallas_call(
        functools.partial(neg_forward_kernel, half),
        grid=(2 * half,),
        in_specs=[
            pl.BlockSpec((2, places, rows), lambda i: (jnp.minimum(i, half - 1), 0, 0)),
            pl.BlockSpec((peers, rows, 128), lambda i: (0, 0, 0)),
            pl.BlockSpec((2, neg, rows), late),
        ],
        out_specs=[pl.BlockSpec((2, neg, rows), late), pl.BlockSpec((2, places, 128), late)],
        out_shape=[
            jax.ShapeDtypeStruct((peers, neg, rows), jnp.float32),
            jax.ShapeDtypeStruct((peers, places, 128), jnp.bfloat16),
        ],
        scratch_shapes=[pltpu.VMEM((peers, places, 128), jnp.bfloat16)],
        compiler_params=pltpu.CompilerParams(vmem_limit_bytes=32 * MIB),
        cost_estimate=pl.CostEstimate(
            flops=4 * peers * places * rows * 128, bytes_accessed=20 * MIB, transcendentals=0
        ),
        name="neg_forward",
    )(hot, w, slots)


def neg_backward_kernel(half, table_ref, w_ref, slot_ref, v_ref, ask_ref, y_ref, sums, q_part):
    step = pl.program_id(0)
    rows = w_ref.shape[1]
    places = table_ref.shape[1]

    @pl.when(step < half)
    def _():
        grads = []
        for part in range(2):
            device = 2 * step + part
            place = lax.broadcasted_iota(jnp.int32, (places, rows), 0)
            weight = jnp.zeros((places, rows), jnp.float32)
            for k in range(slot_ref.shape[1]):
                hit = place == slot_ref[part, k : k + 1, :]
                weight = weight + jnp.where(hit, v_ref[part, k : k + 1, :], 0.0)
            weight = weight.astype(jnp.bfloat16)
            q_part[device] = lax.dot_general(
                weight, table_ref[part], (((0,), (0,)), ((), ())), preferred_element_type=jnp.float32
            )
            rows_back = jnp.dot(weight, w_ref[device], preferred_element_type=jnp.float32) / TEMP
            grads.append(rows_back.reshape(-1, SLOTS, 128))
        both = jnp.concatenate(grads, axis=1).astype(jnp.bfloat16)
        sums[:, pl.ds(pl.multiple_of(step * 16, 16), 16), :] = both

    @pl.when(step >= half)
    def _():
        for part in range(2):
            owner = 2 * (step - half) + part
            target = lax.broadcasted_iota(jnp.int32, (rows, places), 0)
            hot = jnp.where(target == ask_ref[part], 1.0, 0.0).astype(jnp.bfloat16)
            p_grad = jnp.dot(hot, sums[owner], preferred_element_type=jnp.float32)
            lane = lax.broadcasted_iota(jnp.int32, p_grad.shape, 1)
            y_ref[part] = jnp.where(lane < 64, p_grad, q_part[owner] / TEMP).astype(jnp.bfloat16)


def neg_backward(table, w, slots, v, asked):
    peers, places, _ = table.shape
    rows = w.shape[1]
    neg = slots.shape[1]
    half = peers // 2
    early = lambda i: (jnp.minimum(i, half - 1), 0, 0)
    late = lambda i: (jnp.maximum(i - half, 0), 0, 0)
    return pl.pallas_call(
        functools.partial(neg_backward_kernel, half),
        grid=(2 * half,),
        in_specs=[
            pl.BlockSpec((2, places, 128), early),
            pl.BlockSpec((peers, rows, 128), lambda i: (0, 0, 0)),
            pl.BlockSpec((2, neg, rows), early),
            pl.BlockSpec((2, neg, rows), early),
            pl.BlockSpec((2, 1, places), late),
        ],
        out_specs=pl.BlockSpec((2, rows, 128), late),
        out_shape=jax.ShapeDtypeStruct((peers, rows, 128), jnp.bfloat16),
        scratch_shapes=[
            pltpu.VMEM((peers, places, 128), jnp.bfloat16),
            pltpu.VMEM((peers, rows, 128), jnp.float32),
        ],
        compiler_params=pltpu.CompilerParams(vmem_limit_bytes=40 * MIB),
        cost_estimate=pl.CostEstimate(
            flops=6 * peers * places * rows * 128, bytes_accessed=14 * MIB, transcendentals=0
        ),
        name="neg_backward",
    )(table, w, slots, v, asked)


def window_kernel(w_ref, z_ref, *refs):
    q_refs, p_refs, (q_out, p_out) = refs[:STOPS], refs[STOPS : 2 * STOPS], refs[2 * STOPS :]
    rows = w_ref.shape[0]
    q_grad = jnp.zeros(q_out.shape, jnp.float32)
    p_grad = jnp.zeros(p_out.shape, jnp.float32)
    for stop in range(STOPS):
        weight = w_ref[:, stop * rows : (stop + 1) * rows]
        q_grad = q_grad + jnp.dot(weight, p_refs[stop][...], preferred_element_type=jnp.float32)
        p_grad = p_grad + lax.dot_general(
            z_ref[stop], q_refs[stop][...], (((0,), (0,)), ((), ())), preferred_element_type=jnp.float32
        )
    q_out[...] = q_grad / TEMP
    p_out[...] = p_grad / TEMP


def window_grads(weight, back, q_blocks, p_blocks):
    rows, width = q_blocks[0].shape
    step = 512
    tile = pl.BlockSpec((rows, step), lambda i: (0, i))
    return pl.pallas_call(
        window_kernel,
        grid=(width // step,),
        in_specs=[
            pl.BlockSpec((rows, STOPS * rows), lambda i: (0, 0)),
            pl.BlockSpec((STOPS, rows, rows), lambda i: (0, 0, 0)),
        ]
        + [tile] * (2 * STOPS),
        out_specs=[tile, tile],
        out_shape=[jax.ShapeDtypeStruct((rows, width), jnp.float32)] * 2,
        compiler_params=pltpu.CompilerParams(vmem_limit_bytes=32 * MIB),
        cost_estimate=pl.CostEstimate(
            flops=4 * STOPS * rows * rows * width, bytes_accessed=12 * MIB, transcendentals=0
        ),
        name="window_grads",
    )(weight, back, *q_blocks, *p_blocks)


def final_kernel(q_ref, p_ref, gain_ref, qn_ref, pn_ref, qg_ref, pg_ref, y_ref, q_out, p_out, gain_out, q_all, p_all):
    width = q_ref.shape[1]
    low = lax.broadcasted_iota(jnp.int32, (q_ref.shape[0], 128), 1) < 64
    for tile in range(width // 128):
        cut = slice(tile * 128, (tile + 1) * 128)
        even = y_ref[2 * tile].astype(jnp.float32)
        odd = y_ref[2 * tile + 1].astype(jnp.float32)
        p_all[:, cut] = pg_ref[:, cut] + jnp.where(low, even, pltpu.roll(odd, 64, 1))
        q_all[:, cut] = qg_ref[:, cut] + jnp.where(low, pltpu.roll(even, 64, 1), odd)
    gain = gain_ref[...]
    total = jnp.zeros((1, width), jnp.float32)
    for src, norm, grads, out in ((q_ref, qn_ref, q_all, q_out), (p_ref, pn_ref, p_all, p_out)):
        hidden = src[...].astype(jnp.float32)
        inverse = 1.0 / norm[:, :1]
        unit = hidden * gain * inverse
        grad = grads[...]
        inner = jnp.sum(unit * grad, axis=-1, keepdims=True)
        scaled = (grad - unit * inner) * inverse
        out[...] = scaled * gain
        total = total + jnp.sum(hidden * scaled, axis=0, keepdims=True)

    @pl.when(pl.program_id(0) == 0)
    def _():
        gain_out[...] = jnp.zeros_like(gain_out)

    gain_out[...] += total


def finish(q_hidden, p_hidden, gain, q_norm, p_norm, q_grad, p_grad, y):
    rows, width = q_hidden.shape
    step = 32
    row_block = pl.BlockSpec((step, width), lambda i: (i, 0))
    norm_block = pl.BlockSpec((step, 128), lambda i: (i, 0))
    gain_block = pl.BlockSpec((1, width), lambda i: (0, 0))
    return pl.pallas_call(
        final_kernel,
        grid=(rows // step,),
        in_specs=[
            row_block,
            row_block,
            gain_block,
            norm_block,
            norm_block,
            row_block,
            row_block,
            pl.BlockSpec((width // 64, step, 128), lambda i: (0, i, 0)),
        ],
        out_specs=[row_block, row_block, gain_block],
        out_shape=[
            jax.ShapeDtypeStruct((rows, width), jnp.float32),
            jax.ShapeDtypeStruct((rows, width), jnp.float32),
            jax.ShapeDtypeStruct((1, width), jnp.float32),
        ],
        scratch_shapes=[pltpu.VMEM((step, width), jnp.float32)] * 2,
        compiler_params=pltpu.CompilerParams(vmem_limit_bytes=40 * MIB),
        cost_estimate=pl.CostEstimate(flops=20 * rows * width, bytes_accessed=24 * rows * width, transcendentals=0),
        name="finish",
    )(q_hidden, p_hidden, gain.reshape(1, width), q_norm, p_norm, q_grad, p_grad, y)


def slot_tables(wanted, peers):
    rows, neg = wanted.shape
    flat = wanted.T.reshape(-1)
    count = flat.shape[0]
    owner = flat // rows
    place = jnp.arange(count, dtype=jnp.int32)
    same = flat[:, None] == flat[None, :]
    again = jnp.any(same & (place[None, :] < place[:, None]), axis=1)
    smaller = (owner[:, None] == owner[None, :]) & (flat[:, None] < flat[None, :])
    rank = jnp.sum((smaller & ~again[:, None]).astype(jnp.int32), axis=0)
    slot = owner * SLOTS + rank
    table = jnp.arange(peers * SLOTS, dtype=jnp.int32)
    hit = (slot[None, :] == table[:, None]) & ~again[None, :]
    named = jnp.sum(jnp.where(hit, flat[None, :] % rows + 1, 0), axis=1) - 1
    return slot, named


def local(query_hidden, passage_hidden, norm_gain, negatives):
    q_hidden, p_hidden, wanted = query_hidden[0], passage_hidden[0], negatives[0]
    rows, width = q_hidden.shape
    neg = wanted.shape[1]
    peers = lax.axis_size("batch")
    me = lax.axis_index("batch")

    q_emb, p_emb, tiles, q_norm, p_norm = normalize(q_hidden, p_hidden, norm_gain)
    w = lax.all_to_all(tiles, "batch", split_axis=0, concat_axis=0, tiled=True)

    slot, named = slot_tables(wanted, peers)
    tables = lax.all_gather(jnp.concatenate([named, slot]), "batch")
    named_all = tables[:, : peers * SLOTS].reshape(peers, peers, SLOTS)
    asked = named_all.transpose(1, 0, 2).reshape(peers, peers * SLOTS)
    slots = tables[:, peers * SLOTS :].reshape(peers, neg, rows)
    hot = (asked[:, :, None] == jnp.arange(rows, dtype=jnp.int32)).astype(jnp.bfloat16)

    p_blocks, q_blocks = [p_emb], [q_emb]
    for _ in range(1, STOPS):
        p_blocks.append(from_behind(p_blocks[-1], "batch", 1))
        q_blocks.append(from_behind(q_blocks[-1], "batch", -1))

    t_part, neg_table = neg_forward(hot, w, slots)
    t_parts = lax.all_to_all(t_part, "batch", split_axis=0, concat_axis=0, tiled=True)
    neg_scores = jnp.sum(t_parts, axis=0) / TEMP

    scores = jnp.concatenate(
        [jnp.dot(q_emb, block.T, preferred_element_type=jnp.float32) for block in p_blocks], axis=1
    ) / TEMP
    exp_scores = jnp.exp(scores)
    exp_negative = jnp.exp(neg_scores)
    partition = jnp.sum(exp_scores, axis=1) + jnp.sum(exp_negative, axis=0)
    inverse = 1.0 / partition
    query_loss = jnp.log(partition) - jnp.diagonal(scores[:, :rows])
    identity = jnp.eye(rows, STOPS * rows, dtype=jnp.float32)
    weight = (exp_scores * inverse[:, None] - identity).astype(jnp.bfloat16)
    neg_weight = (exp_negative * inverse[None, :]).astype(jnp.bfloat16).astype(jnp.float32)

    shared = lax.all_gather(jnp.concatenate([neg_weight, inverse[None, :]], axis=0), "batch")
    y = neg_backward(neg_table, w, slots, shared[:, :neg], asked[:, None, :])
    y_back = lax.all_to_all(y, "batch", split_axis=0, concat_axis=0, tiled=True)

    back = [weight[:, :rows]]
    for stop in range(1, STOPS):
        others = jnp.exp(jnp.dot(q_blocks[stop], p_emb.T, preferred_element_type=jnp.float32) / TEMP)
        their_inverse = lax.dynamic_index_in_dim(shared[:, neg], (me + stop) % peers, keepdims=False)
        back.append((others * their_inverse[:, None]).astype(jnp.bfloat16))
    q_grad, p_grad = window_grads(weight, jnp.stack(back), q_blocks, p_blocks)

    query_grad, passage_grad, gain_part = finish(
        q_hidden, p_hidden, norm_gain, q_norm, p_norm, q_grad, p_grad, y_back
    )
    gain_grad = lax.psum(gain_part[0], ("batch", "rep"))
    return (query_grad[None], passage_grad[None], query_loss[None], gain_grad)


def solution(mesh):
    return jax.shard_map(
        local,
        mesh=mesh,
        in_specs=(P("rep", "batch", None), P("rep", "batch", None), P(), P("rep", "batch", None)),
        out_specs=(P("rep", "batch", None), P("rep", "batch", None), P("rep", "batch"), P()),
        check_vma=False,
    )
```

```python
import functools

import jax
import jax.numpy as jnp
from jax import lax
from jax.experimental import pallas as pl
from jax.experimental.pallas import tpu as pltpu
from jax.sharding import PartitionSpec as P

STOPS = 4
TEMP = 0.05
EPS = 1e-06
SLOTS = 8
MIB = 1 << 20


def from_behind(block, axis, distance):
    size = lax.axis_size(axis)
    route = [((i - distance) % size, i) for i in range(size)]
    return lax.ppermute(block, axis, route)


def norm_kernel(q_ref, p_ref, gain_ref, qe_ref, pe_ref, x_ref, qn_ref, pn_ref):
    gain = gain_ref[...]
    units = []
    for src, emb, norm in ((q_ref, qe_ref, qn_ref), (p_ref, pe_ref, pn_ref)):
        scaled = src[...].astype(jnp.float32) * gain
        length = jnp.sqrt(jnp.sum(scaled * scaled, axis=-1, keepdims=True) + EPS)
        unit = scaled * (1.0 / length)
        emb[...] = unit.astype(jnp.bfloat16)
        norm[...] = jnp.broadcast_to(length, norm.shape)
        units.append(unit)
    q_unit, p_unit = units
    low = lax.broadcasted_iota(jnp.int32, (q_ref.shape[0], 128), 1) < 64
    for tile in range(q_ref.shape[1] // 128):
        q_tile = q_unit[:, tile * 128 : (tile + 1) * 128]
        p_tile = p_unit[:, tile * 128 : (tile + 1) * 128]
        x_ref[2 * tile] = jnp.where(low, q_tile, pltpu.roll(p_tile, 64, 1)).astype(jnp.bfloat16)
        x_ref[2 * tile + 1] = jnp.where(low, pltpu.roll(q_tile, 64, 1), p_tile).astype(jnp.bfloat16)


def normalize(q_hidden, p_hidden, gain):
    rows, width = q_hidden.shape
    tiles = width // 64
    step = 32
    row_block = pl.BlockSpec((step, width), lambda i: (i, 0))
    norm_block = pl.BlockSpec((step, 128), lambda i: (i, 0))
    return pl.pallas_call(
        norm_kernel,
        grid=(rows // step,),
        in_specs=[row_block, row_block, pl.BlockSpec((1, width), lambda i: (0, 0))],
        out_specs=[
            row_block,
            row_block,
            pl.BlockSpec((tiles, step, 128), lambda i: (0, i, 0)),
            norm_block,
            norm_block,
        ],
        out_shape=[
            jax.ShapeDtypeStruct((rows, width), jnp.bfloat16),
            jax.ShapeDtypeStruct((rows, width), jnp.bfloat16),
            jax.ShapeDtypeStruct((tiles, rows, 128), jnp.bfloat16),
            jax.ShapeDtypeStruct((rows, 128), jnp.float32),
            jax.ShapeDtypeStruct((rows, 128), jnp.float32),
        ],
        compiler_params=pltpu.CompilerParams(vmem_limit_bytes=32 * MIB),
        cost_estimate=pl.CostEstimate(flops=10 * rows * width, bytes_accessed=10 * rows * width, transcendentals=0),
        name="normalize",
    )(q_hidden, p_hidden, gain.reshape(1, width))


def neg_forward_kernel(half, hot_ref, w_ref, slot_ref, t_ref, table_ref, scratch):
    step = pl.program_id(0)

    @pl.when(step < half)
    def _():
        picked = []
        for part in range(2):
            rows = jnp.dot(hot_ref[part], w_ref[2 * step + part], preferred_element_type=jnp.float32)
            picked.append(rows.reshape(-1, SLOTS, 128))
        both = jnp.concatenate(picked, axis=1).astype(jnp.bfloat16)
        scratch[:, pl.ds(pl.multiple_of(step * 16, 16), 16), :] = both

    @pl.when(step >= half)
    def _():
        pair = step - half
        for part in range(2):
            device = 2 * pair + part
            table = scratch[device]
            table_ref[part] = table
            mine = w_ref[device].astype(jnp.float32)
            lane = lax.broadcasted_iota(jnp.int32, mine.shape, 1)
            query = jnp.where(lane < 64, 0.0, pltpu.roll(mine, 64, 1)).astype(jnp.bfloat16)
            scores = lax.dot_general(
                table, query, (((1,), (1,)), ((), ())), preferred_element_type=jnp.float32
            )
            place = lax.broadcasted_iota(jnp.int32, scores.shape, 0)
            for k in range(t_ref.shape[1]):
                hit = place == slot_ref[part, k : k + 1, :]
                t_ref[part, k : k + 1, :] = jnp.sum(jnp.where(hit, scores, 0.0), axis=0, keepdims=True)


def neg_forward(hot, w, slots):
    peers, places, rows = hot.shape
    neg = slots.shape[1]
    half = peers // 2
    late = lambda i: (jnp.maximum(i - half, 0), 0, 0)
    return pl.pallas_call(
        functools.partial(neg_forward_kernel, half),
        grid=(2 * half,),
        in_specs=[
            pl.BlockSpec((2, places, rows), lambda i: (jnp.minimum(i, half - 1), 0, 0)),
            pl.BlockSpec((peers, rows, 128), lambda i: (0, 0, 0)),
            pl.BlockSpec((2, neg, rows), late),
        ],
        out_specs=[pl.BlockSpec((2, neg, rows), late), pl.BlockSpec((2, places, 128), late)],
        out_shape=[
            jax.ShapeDtypeStruct((peers, neg, rows), jnp.float32),
            jax.ShapeDtypeStruct((peers, places, 128), jnp.bfloat16),
        ],
        scratch_shapes=[pltpu.VMEM((peers, places, 128), jnp.bfloat16)],
        compiler_params=pltpu.CompilerParams(vmem_limit_bytes=32 * MIB),
        cost_estimate=pl.CostEstimate(
            flops=4 * peers * places * rows * 128, bytes_accessed=20 * MIB, transcendentals=0
        ),
        name="neg_forward",
    )(hot, w, slots)


def neg_backward_kernel(half, table_ref, w_ref, slot_ref, v_ref, ask_ref, y_ref, sums, q_part):
    step = pl.program_id(0)
    rows = w_ref.shape[1]
    places = table_ref.shape[1]

    @pl.when(step < half)
    def _():
        grads = []
        for part in range(2):
            device = 2 * step + part
            place = lax.broadcasted_iota(jnp.int32, (places, rows), 0)
            weight = jnp.zeros((places, rows), jnp.float32)
            for k in range(slot_ref.shape[1]):
                hit = place == slot_ref[part, k : k + 1, :]
                weight = weight + jnp.where(hit, v_ref[part, k : k + 1, :], 0.0)
            weight = weight.astype(jnp.bfloat16)
            q_part[device] = lax.dot_general(
                weight, table_ref[part], (((0,), (0,)), ((), ())), preferred_element_type=jnp.float32
            )
            rows_back = jnp.dot(weight, w_ref[device], preferred_element_type=jnp.float32) / TEMP
            grads.append(rows_back.reshape(-1, SLOTS, 128))
        both = jnp.concatenate(grads, axis=1).astype(jnp.bfloat16)
        sums[:, pl.ds(pl.multiple_of(step * 16, 16), 16), :] = both

    @pl.when(step >= half)
    def _():
        for part in range(2):
            owner = 2 * (step - half) + part
            target = lax.broadcasted_iota(jnp.int32, (rows, places), 0)
            hot = jnp.where(target == ask_ref[part], 1.0, 0.0).astype(jnp.bfloat16)
            p_grad = jnp.dot(hot, sums[owner], preferred_element_type=jnp.float32)
            lane = lax.broadcasted_iota(jnp.int32, p_grad.shape, 1)
            y_ref[part] = jnp.where(lane < 64, p_grad, q_part[owner] / TEMP).astype(jnp.bfloat16)


def neg_backward(table, w, slots, v, asked):
    peers, places, _ = table.shape
    rows = w.shape[1]
    neg = slots.shape[1]
    half = peers // 2
    early = lambda i: (jnp.minimum(i, half - 1), 0, 0)
    late = lambda i: (jnp.maximum(i - half, 0), 0, 0)
    return pl.pallas_call(
        functools.partial(neg_backward_kernel, half),
        grid=(2 * half,),
        in_specs=[
            pl.BlockSpec((2, places, 128), early),
            pl.BlockSpec((peers, rows, 128), lambda i: (0, 0, 0)),
            pl.BlockSpec((2, neg, rows), early),
            pl.BlockSpec((2, neg, rows), early),
            pl.BlockSpec((2, 1, places), late),
        ],
        out_specs=pl.BlockSpec((2, rows, 128), late),
        out_shape=jax.ShapeDtypeStruct((peers, rows, 128), jnp.bfloat16),
        scratch_shapes=[
            pltpu.VMEM((peers, places, 128), jnp.bfloat16),
            pltpu.VMEM((peers, rows, 128), jnp.float32),
        ],
        compiler_params=pltpu.CompilerParams(vmem_limit_bytes=40 * MIB),
        cost_estimate=pl.CostEstimate(
            flops=6 * peers * places * rows * 128, bytes_accessed=14 * MIB, transcendentals=0
        ),
        name="neg_backward",
    )(table, w, slots, v, asked)


def window_kernel(w_ref, z_ref, *refs):
    q_refs, p_refs, (q_out, p_out) = refs[:STOPS], refs[STOPS : 2 * STOPS], refs[2 * STOPS :]
    rows = w_ref.shape[0]
    q_grad = jnp.zeros(q_out.shape, jnp.float32)
    p_grad = jnp.zeros(p_out.shape, jnp.float32)
    for stop in range(STOPS):
        weight = w_ref[:, stop * rows : (stop + 1) * rows]
        q_grad = q_grad + jnp.dot(weight, p_refs[stop][...], preferred_element_type=jnp.float32)
        p_grad = p_grad + lax.dot_general(
            z_ref[stop], q_refs[stop][...], (((0,), (0,)), ((), ())), preferred_element_type=jnp.float32
        )
    q_out[...] = q_grad / TEMP
    p_out[...] = p_grad / TEMP


def window_grads(weight, back, q_blocks, p_blocks):
    rows, width = q_blocks[0].shape
    step = 512
    tile = pl.BlockSpec((rows, step), lambda i: (0, i))
    return pl.pallas_call(
        window_kernel,
        grid=(width // step,),
        in_specs=[
            pl.BlockSpec((rows, STOPS * rows), lambda i: (0, 0)),
            pl.BlockSpec((STOPS, rows, rows), lambda i: (0, 0, 0)),
        ]
        + [tile] * (2 * STOPS),
        out_specs=[tile, tile],
        out_shape=[jax.ShapeDtypeStruct((rows, width), jnp.float32)] * 2,
        compiler_params=pltpu.CompilerParams(vmem_limit_bytes=32 * MIB),
        cost_estimate=pl.CostEstimate(
            flops=4 * STOPS * rows * rows * width, bytes_accessed=12 * MIB, transcendentals=0
        ),
        name="window_grads",
    )(weight, back, *q_blocks, *p_blocks)


def final_kernel(q_ref, p_ref, gain_ref, qn_ref, pn_ref, qg_ref, pg_ref, y_ref, q_out, p_out, gain_out, q_all, p_all):
    width = q_ref.shape[1]
    low = lax.broadcasted_iota(jnp.int32, (q_ref.shape[0], 128), 1) < 64
    for tile in range(width // 128):
        cut = slice(tile * 128, (tile + 1) * 128)
        even = y_ref[2 * tile].astype(jnp.float32)
        odd = y_ref[2 * tile + 1].astype(jnp.float32)
        p_all[:, cut] = pg_ref[:, cut] + jnp.where(low, even, pltpu.roll(odd, 64, 1))
        q_all[:, cut] = qg_ref[:, cut] + jnp.where(low, pltpu.roll(even, 64, 1), odd)
    gain = gain_ref[...]
    total = jnp.zeros((1, width), jnp.float32)
    for src, norm, grads, out in ((q_ref, qn_ref, q_all, q_out), (p_ref, pn_ref, p_all, p_out)):
        hidden = src[...].astype(jnp.float32)
        inverse = 1.0 / norm[:, :1]
        unit = hidden * gain * inverse
        grad = grads[...]
        inner = jnp.sum(unit * grad, axis=-1, keepdims=True)
        scaled = (grad - unit * inner) * inverse
        out[...] = scaled * gain
        total = total + jnp.sum(hidden * scaled, axis=0, keepdims=True)

    @pl.when(pl.program_id(0) == 0)
    def _():
        gain_out[...] = jnp.zeros_like(gain_out)

    gain_out[...] += total


def finish(q_hidden, p_hidden, gain, q_norm, p_norm, q_grad, p_grad, y):
    rows, width = q_hidden.shape
    step = 32
    row_block = pl.BlockSpec((step, width), lambda i: (i, 0))
    norm_block = pl.BlockSpec((step, 128), lambda i: (i, 0))
    gain_block = pl.BlockSpec((1, width), lambda i: (0, 0))
    return pl.pallas_call(
        final_kernel,
        grid=(rows // step,),
        in_specs=[
            row_block,
            row_block,
            gain_block,
            norm_block,
            norm_block,
            row_block,
            row_block,
            pl.BlockSpec((width // 64, step, 128), lambda i: (0, i, 0)),
        ],
        out_specs=[row_block, row_block, gain_block],
        out_shape=[
            jax.ShapeDtypeStruct((rows, width), jnp.float32),
            jax.ShapeDtypeStruct((rows, width), jnp.float32),
            jax.ShapeDtypeStruct((1, width), jnp.float32),
        ],
        scratch_shapes=[pltpu.VMEM((step, width), jnp.float32)] * 2,
        compiler_params=pltpu.CompilerParams(vmem_limit_bytes=40 * MIB),
        cost_estimate=pl.CostEstimate(flops=20 * rows * width, bytes_accessed=24 * rows * width, transcendentals=0),
        name="finish",
    )(q_hidden, p_hidden, gain.reshape(1, width), q_norm, p_norm, q_grad, p_grad, y)


MESH = pl.DeviceIdType.MESH
LINE = 8


def rounds(me, rep, peers, reps):
    z, line = lax.rem(me, LINE), me // LINE
    return (
        (z, LINE, lambda i: (line * LINE + i, rep)),
        (line, peers // LINE, lambda i: (i * LINE + z, rep)),
        (rep, reps, lambda i: (me, i)),
    )


def sum_kernel(peers, reps, part_ref, out_ref, slots, send_sems, recv_sems):
    me, rep = lax.axis_index("batch"), lax.axis_index("rep")
    plan = rounds(me, rep, peers, reps)
    barrier = pltpu.get_barrier_semaphore()
    total = 0
    for here, size, target in plan:
        for off in range(1, size):
            pl.semaphore_signal(barrier, inc=1, device_id=target(lax.rem(here + off, size)), device_id_type=MESH)
            total += 1
    pl.semaphore_wait(barrier, total)
    out_ref[...] = part_ref[...]
    for turn, (here, size, target) in enumerate(plan):
        slots[turn, here] = out_ref[...]
        copies = []
        for off in range(1, size):
            copies.append(
                pltpu.make_async_remote_copy(
                    src_ref=slots.at[turn, here],
                    dst_ref=slots.at[turn, here],
                    send_sem=send_sems.at[turn, off],
                    recv_sem=recv_sems.at[turn, here],
                    device_id=target(lax.rem(here + off, size)),
                    device_id_type=MESH,
                )
            )
            copies[-1].start()
        for off in range(1, size):
            other = lax.rem(here + off, size)
            pltpu.make_async_remote_copy(
                src_ref=slots.at[turn, other],
                dst_ref=slots.at[turn, other],
                send_sem=send_sems.at[turn, off],
                recv_sem=recv_sems.at[turn, other],
                device_id=target(other),
                device_id_type=MESH,
            ).wait_recv()
        total = slots[turn, 0]
        for i in range(1, size):
            total = total + slots[turn, i]
        out_ref[...] = total
        for copy in copies:
            copy.wait_send()


def sum_over_devices(part):
    peers, reps = lax.axis_size("batch"), lax.axis_size("rep")
    width = part.shape[-1]
    shape = (width // 128, 128)
    most = max(LINE, peers // LINE, reps)
    out = pl.pallas_call(
        functools.partial(sum_kernel, peers, reps),
        in_specs=[pl.BlockSpec(memory_space=pltpu.VMEM)],
        out_specs=pl.BlockSpec(memory_space=pltpu.VMEM),
        out_shape=jax.ShapeDtypeStruct(shape, jnp.float32),
        scratch_shapes=[
            pltpu.VMEM((3, most) + shape, jnp.float32),
            pltpu.SemaphoreType.DMA((3, most)),
            pltpu.SemaphoreType.DMA((3, most)),
        ],
        compiler_params=pltpu.CompilerParams(collective_id=0, has_side_effects=True),
        name="gain_sum",
    )(part.reshape(shape))
    return out.reshape(width)


def to_all(part):
    peers = lax.axis_size("batch")
    return lax.all_to_all(
        jnp.broadcast_to(part[None], (peers,) + part.shape), "batch", split_axis=0, concat_axis=0, tiled=True
    )


def slot_tables(wanted, peers):
    rows, neg = wanted.shape
    flat = wanted.T.reshape(-1)
    count = flat.shape[0]
    owner = flat // rows
    place = jnp.arange(count, dtype=jnp.int32)
    same = flat[:, None] == flat[None, :]
    again = jnp.any(same & (place[None, :] < place[:, None]), axis=1)
    smaller = (owner[:, None] == owner[None, :]) & (flat[:, None] < flat[None, :])
    rank = jnp.sum((smaller & ~again[:, None]).astype(jnp.int32), axis=0)
    slot = owner * SLOTS + rank
    table = jnp.arange(peers * SLOTS, dtype=jnp.int32)
    hit = (slot[None, :] == table[:, None]) & ~again[None, :]
    named = jnp.sum(jnp.where(hit, flat[None, :] % rows + 1, 0), axis=1) - 1
    return slot, named


def local(query_hidden, passage_hidden, norm_gain, negatives):
    q_hidden, p_hidden, wanted = query_hidden[0], passage_hidden[0], negatives[0]
    rows, width = q_hidden.shape
    neg = wanted.shape[1]
    peers = lax.axis_size("batch")
    me = lax.axis_index("batch")

    q_emb, p_emb, tiles, q_norm, p_norm = normalize(q_hidden, p_hidden, norm_gain)
    w = lax.all_to_all(tiles, "batch", split_axis=0, concat_axis=0, tiled=True)

    slot, named = slot_tables(wanted, peers)
    tables = to_all(jnp.concatenate([named, slot]))
    named_all = tables[:, : peers * SLOTS].reshape(peers, peers, SLOTS)
    asked = named_all.transpose(1, 0, 2).reshape(peers, peers * SLOTS)
    slots = tables[:, peers * SLOTS :].reshape(peers, neg, rows)
    hot = (asked[:, :, None] == jnp.arange(rows, dtype=jnp.int32)).astype(jnp.bfloat16)

    p_blocks, q_blocks = [p_emb], [q_emb]
    for _ in range(1, STOPS):
        p_blocks.append(from_behind(p_blocks[-1], "batch", 1))
        q_blocks.append(from_behind(q_blocks[-1], "batch", -1))

    t_part, neg_table = neg_forward(hot, w, slots)
    t_parts = lax.all_to_all(t_part, "batch", split_axis=0, concat_axis=0, tiled=True)
    neg_scores = jnp.sum(t_parts, axis=0) / TEMP

    scores = jnp.concatenate(
        [jnp.dot(q_emb, block.T, preferred_element_type=jnp.float32) for block in p_blocks], axis=1
    ) / TEMP
    exp_scores = jnp.exp(scores)
    exp_negative = jnp.exp(neg_scores)
    partition = jnp.sum(exp_scores, axis=1) + jnp.sum(exp_negative, axis=0)
    inverse = 1.0 / partition
    query_loss = jnp.log(partition) - jnp.diagonal(scores[:, :rows])
    identity = jnp.eye(rows, STOPS * rows, dtype=jnp.float32)
    weight = (exp_scores * inverse[:, None] - identity).astype(jnp.bfloat16)
    neg_weight = (exp_negative * inverse[None, :]).astype(jnp.bfloat16).astype(jnp.float32)

    shared = to_all(jnp.concatenate([neg_weight, inverse[None, :]], axis=0))
    y = neg_backward(neg_table, w, slots, shared[:, :neg], asked[:, None, :])
    y_back = lax.all_to_all(y, "batch", split_axis=0, concat_axis=0, tiled=True)

    back = [weight[:, :rows]]
    for stop in range(1, STOPS):
        others = jnp.exp(jnp.dot(q_blocks[stop], p_emb.T, preferred_element_type=jnp.float32) / TEMP)
        their_inverse = lax.dynamic_index_in_dim(shared[:, neg], (me + stop) % peers, keepdims=False)
        back.append((others * their_inverse[:, None]).astype(jnp.bfloat16))
    q_grad, p_grad = window_grads(weight, jnp.stack(back), q_blocks, p_blocks)

    query_grad, passage_grad, gain_part = finish(
        q_hidden, p_hidden, norm_gain, q_norm, p_norm, q_grad, p_grad, y_back
    )
    gain_grad = sum_over_devices(gain_part)
    return (query_grad[None], passage_grad[None], query_loss[None], gain_grad)


def solution(mesh):
    return jax.shard_map(
        local,
        mesh=mesh,
        in_specs=(P("rep", "batch", None), P("rep", "batch", None), P(), P("rep", "batch", None)),
        out_specs=(P("rep", "batch", None), P("rep", "batch", None), P("rep", "batch"), P()),
        check_vma=False,
    )
```

```python
import functools

import jax
import jax.numpy as jnp
from jax import lax
from jax.experimental import pallas as pl
from jax.experimental.pallas import tpu as pltpu
from jax.sharding import PartitionSpec as P

STOPS = 4
TEMP = 0.05
EPS = 1e-06
SLOTS = 8
LINE = 8
STRIDE, UNSTRIDE = 27, 19
HOP_STEP = 20
MIB = 1 << 20
MESH = pl.DeviceIdType.MESH
NT = (((1,), (1,)), ((), ()))
TN = (((0,), (0,)), ((), ()))


def dot(a, b, dims=(((1,), (0,)), ((), ()))):
    return lax.dot_general(a, b, dims, preferred_element_type=jnp.float32)


def kernel(
    n, reps, q_ref, p_ref, gain_ref, idx_ref, q_out, p_out, loss_ref, gain_out,
    p_win, q_win, x_send, w, y_send, y_recv, table, sums, q_part, idx_all, asks, asks_t, t_send, t_recv,
    shared, side_send, side_recv, q_norm, p_norm, q_weight, p_weight, gain_slots,
    x_sem, x_sems, idx_sem, idx_got, t_sem, t_got, sh_sem, sh_got, y_sem, y_got,
    chain_sem, chain_got, side_sem, side_got, g_sems, g_got,
):
    me, rep = lax.axis_index("batch"), lax.axis_index("rep")
    rows, width = q_ref.shape
    neg = 3
    places = n * SLOTS

    def ahead(i):
        return lax.rem(me + STRIDE * i, n)

    def behind(i):
        return lax.rem(me + n * STRIDE - STRIDE * i, n)

    def position(device):
        return lax.rem((me + n - device) * UNSTRIDE, n)

    def remote(src, dst, send, recv, device):
        return pltpu.make_async_remote_copy(
            src_ref=src, dst_ref=dst, send_sem=send, recv_sem=recv, device_id=(device, rep), device_id_type=MESH
        )

    barrier = pltpu.get_barrier_semaphore()

    def greet(i, carry):
        pl.semaphore_signal(barrier, inc=1, device_id=(ahead(i), rep), device_id_type=MESH)
        return carry

    lax.fori_loop(1, n, greet, 0)
    for off in range(1, reps):
        pl.semaphore_signal(barrier, inc=1, device_id=(me, lax.rem(rep + off, reps)), device_id_type=MESH)

    def normalize(chunk, carry):
        cut = pl.ds(pl.multiple_of(chunk * 16, 16), 16)
        units = []
        for src, win, norm in ((q_ref, q_win, q_norm), (p_ref, p_win, p_norm)):
            scaled = src[cut, :].astype(jnp.float32) * gain_ref[...]
            length = jnp.sqrt(jnp.sum(scaled * scaled, axis=-1, keepdims=True) + EPS)
            unit = scaled * (1.0 / length)
            win[0, cut, :] = unit.astype(jnp.bfloat16)
            norm[cut, :] = jnp.broadcast_to(1.0 / length, (16, 128))
            units.append(unit)
        low = lax.broadcasted_iota(jnp.int32, (16, 128), 1) < 64
        for tile in range(width // 128):
            q_tile = units[0][:, tile * 128 : (tile + 1) * 128]
            p_tile = units[1][:, tile * 128 : (tile + 1) * 128]
            x_send[2 * tile, cut, :] = jnp.where(low, q_tile, pltpu.roll(p_tile, 64, 1)).astype(jnp.bfloat16)
            x_send[2 * tile + 1, cut, :] = jnp.where(low, pltpu.roll(q_tile, 64, 1), p_tile).astype(jnp.bfloat16)
        return carry

    lax.fori_loop(0, rows // 16, normalize, 0)
    idx_all[0] = idx_ref[...]
    w[0] = x_send[me]
    pl.semaphore_wait(barrier, n - 1 + reps - 1)

    def idx_copy(i):
        return remote(idx_all.at[0], idx_all.at[i], idx_sem, idx_got, ahead(i))

    def x_copy(i):
        return remote(x_send.at[ahead(i)], w.at[i], x_sem, x_sems.at[i], ahead(i))

    def start_idx(i, carry):
        idx_copy(i).start()
        return carry

    def start_x(i, carry):
        x_copy(i).start()
        return carry

    right, left = lax.rem(me + 1, n), lax.rem(me + n - 1, n)

    def hop(turn):
        return (
            remote(p_win.at[turn - 1], p_win.at[turn], chain_sem.at[0, turn - 1], chain_got.at[0, turn - 1], right),
            remote(q_win.at[turn - 1], q_win.at[turn], chain_sem.at[1, turn - 1], chain_got.at[1, turn - 1], left),
        )

    def pass_on(turn):
        for copy in hop(turn):
            copy.wait_recv()
        if turn + 1 < STOPS:
            for copy in hop(turn + 1):
                copy.start()

    lax.fori_loop(1, n, start_idx, 0)
    for copy in hop(1):
        copy.start()
    lax.fori_loop(1, n, start_x, 0)

    others = pl.ds(1, n - 1)

    def all_others(buffer, send, recv):
        return remote(buffer.at[others], buffer.at[others], send, recv, right)

    all_others(idx_all, idx_sem, idx_got).wait_recv()
    wide = idx_all[:, :SLOTS, :].reshape(places, 128).astype(jnp.float32)
    asks[...] = wide.astype(jnp.bfloat16)
    asks_t[...] = wide.T

    def pick(step, carry):
        @pl.when(step == HOP_STEP * n // 64)
        def _():
            pass_on(1)

        picked = []
        for part in range(2):
            pos = 2 * step + part

            @pl.when(pos > 0)
            def _():
                x_copy(pos).wait_recv()

            owner = behind(pos)
            column = (lax.broadcasted_iota(jnp.int32, (128, 128), 0) == owner).astype(jnp.bfloat16)
            asked = dot(asks[...], column)
            lane = lax.broadcasted_iota(jnp.int32, asked.shape, 1).astype(jnp.float32)
            hot = jnp.where(asked == lane, 1.0, 0.0).astype(jnp.bfloat16)
            picked.append(dot(hot, w[pos]).reshape(n, SLOTS, 128))
        both = jnp.concatenate(picked, axis=1).astype(jnp.bfloat16)
        table[:, pl.ds(pl.multiple_of(step * 16, 16), 16), :] = both
        return carry

    lax.fori_loop(0, n // 2, pick, 0)

    def places_of(pos):
        slot = idx_all[pos, SLOTS : 2 * SLOTS, :]
        turned = ((me + n - (slot >> 3)) * UNSTRIDE) & (n - 1)
        return turned * SLOTS + (slot & (SLOTS - 1))

    def t_copy(pos):
        return remote(t_send.at[pos], t_recv.at[n - pos], t_sem, t_got, behind(pos))

    def partial_scores(pos):
        mine = w[pos].astype(jnp.float32)
        lane = lax.broadcasted_iota(jnp.int32, mine.shape, 1)
        query = jnp.where(lane < 64, 0.0, pltpu.roll(mine, 64, 1)).astype(jnp.bfloat16)
        scores = dot(table[pos], query, NT)
        place = lax.broadcasted_iota(jnp.int32, scores.shape, 0)
        slot = places_of(pos)
        parts = [
            jnp.sum(jnp.where(place == slot[k : k + 1], scores, 0.0), axis=0, keepdims=True) for k in range(neg)
        ]
        return jnp.concatenate(parts + [jnp.zeros((8 - neg, rows), jnp.float32)], axis=0)

    def score_step(pos, carry):
        t_send[pos] = partial_scores(pos)
        t_copy(pos).start()
        return carry

    lax.fori_loop(1, n, score_step, 0)
    t_recv[0] = partial_scores(0)

    def window_scores(p_slot, q_slot):
        step = 512

        def add(tile, total):
            cut = pl.ds(pl.multiple_of(tile * step, step), step)
            return total + dot(p_win[p_slot, :, cut], q_win[q_slot, :, cut], NT)

        return lax.fori_loop(0, width // step, add, jnp.zeros((rows, rows), jnp.float32)) / TEMP

    own = window_scores(0, 0)
    eye = lax.broadcasted_iota(jnp.int32, (rows, rows), 0) == lax.broadcasted_iota(jnp.int32, (rows, rows), 1)
    positive = jnp.sum(jnp.where(eye, own, 0.0), axis=0, keepdims=True)
    exps = [jnp.exp(own), jnp.exp(window_scores(1, 0))]
    pass_on(2)
    far = jnp.sum(jnp.exp(window_scores(2, 1)), axis=0, keepdims=True)
    side_send[...] = jnp.broadcast_to(far, side_send.shape)
    side = remote(side_send, side_recv, side_sem, side_got, right)
    side.start()
    exps.append(jnp.exp(window_scores(2, 0)))
    near = sum(jnp.sum(e, axis=0, keepdims=True) for e in exps)

    all_others(t_recv, t_sem, t_got).wait_recv()
    t = lax.fori_loop(0, n, lambda i, total: total + t_recv[i], jnp.zeros((8, rows), jnp.float32)) / TEMP
    exp_t = jnp.exp(t)
    side.wait_recv()
    partition = near + side_recv[:1] + sum(exp_t[k : k + 1] for k in range(neg))
    inverse = 1.0 / partition
    loss_ref[...] = jnp.log(partition) - positive
    v = (exp_t * inverse).astype(jnp.bfloat16).astype(jnp.float32)
    line = lax.broadcasted_iota(jnp.int32, v.shape, 0)
    shared[0] = jnp.where(line < neg, v, jnp.broadcast_to(inverse, v.shape))

    def sh_copy(i):
        return remote(shared.at[0], shared.at[i], sh_sem, sh_got, ahead(i))

    def start_sh(i, carry):
        sh_copy(i).start()
        return carry

    lax.fori_loop(1, n, start_sh, 0)
    for stop in range(STOPS - 1):
        weight = exps[stop] * inverse
        if stop == 0:
            weight = weight - jnp.where(eye, 1.0, 0.0)
            p_weight[0] = weight.astype(jnp.bfloat16)
        q_weight[stop] = weight.T.astype(jnp.bfloat16)
    all_others(shared, sh_sem, sh_got).wait_recv()

    def spread(step, carry):
        grads = []
        for part in range(2):
            pos = 2 * step + part
            place = lax.broadcasted_iota(jnp.int32, (places, rows), 0)
            slot = places_of(pos)
            weight = jnp.zeros((places, rows), jnp.float32)
            for k in range(neg):
                weight = weight + jnp.where(place == slot[k : k + 1], shared[pos, k : k + 1, :], 0.0)
            weight = weight.astype(jnp.bfloat16)
            q_part[pos] = dot(weight, table[pos], TN)
            grads.append((dot(weight, w[pos]) / TEMP).reshape(n, SLOTS, 128))
        both = jnp.concatenate(grads, axis=1).astype(jnp.bfloat16)
        sums[:, pl.ds(pl.multiple_of(step * 16, 16), 16), :] = both
        return carry

    lax.fori_loop(0, n // 2, spread, 0)

    def y_copy(pos):
        return remote(y_send.at[pos], y_recv.at[n - pos], y_sem, y_got, behind(pos))

    def gather_tile(pos):
        asked = asks_t[pl.ds(behind(pos), 1), :]
        target = lax.broadcasted_iota(jnp.int32, (rows, places), 0).astype(jnp.float32)
        hot = jnp.where(target == asked, 1.0, 0.0).astype(jnp.bfloat16)
        p_grad = dot(hot, sums[pos])
        lane = lax.broadcasted_iota(jnp.int32, p_grad.shape, 1)
        return jnp.where(lane < 64, p_grad, q_part[pos] / TEMP).astype(jnp.bfloat16)

    def gather_step(pos, carry):
        y_send[pos] = gather_tile(pos)
        y_copy(pos).start()
        return carry

    lax.fori_loop(1, n, gather_step, 0)
    y_recv[0] = gather_tile(0)

    pass_on(3)

    def inverse_of(stop):
        return shared[position(lax.rem(me + stop, n)), neg : neg + 1, :]

    for stop in range(1, STOPS):
        p_weight[stop] = (jnp.exp(window_scores(0, stop)) * inverse_of(stop)).astype(jnp.bfloat16)
    q_weight[STOPS - 1] = (jnp.exp(window_scores(STOPS - 1, 0)) * inverse).T.astype(jnp.bfloat16)

    def products(tile, carry):
        cut = pl.ds(pl.multiple_of(tile * 256, 256), 256)
        q_grad = jnp.zeros((rows, 256), jnp.float32)
        p_grad = jnp.zeros((rows, 256), jnp.float32)
        for stop in range(STOPS):
            q_grad = q_grad + dot(q_weight[stop], p_win[stop, :, cut])
            p_grad = p_grad + dot(p_weight[stop], q_win[stop, :, cut])
        q_out[:, cut] = q_grad / TEMP
        p_out[:, cut] = p_grad / TEMP
        return carry

    lax.fori_loop(0, width // 256, products, 0)

    all_others(y_recv, y_sem, y_got).wait_recv()

    def finish(chunk, total):
        cut = pl.ds(pl.multiple_of(chunk * 16, 16), 16)
        low = lax.broadcasted_iota(jnp.int32, (16, 128), 1) < 64
        q_tiles, p_tiles = [], []
        for tile in range(width // 128):
            even = y_recv[position(2 * tile), cut, :].astype(jnp.float32)
            odd = y_recv[position(2 * tile + 1), cut, :].astype(jnp.float32)
            p_tiles.append(jnp.where(low, even, pltpu.roll(odd, 64, 1)))
            q_tiles.append(jnp.where(low, pltpu.roll(even, 64, 1), odd))
        for src, norm, tiles, out in ((q_ref, q_norm, q_tiles, q_out), (p_ref, p_norm, p_tiles, p_out)):
            hidden = src[cut, :].astype(jnp.float32)
            over = norm[cut, :1]
            gain = gain_ref[...]
            unit = hidden * gain * over
            grad = out[cut, :] + jnp.concatenate(tiles, axis=1)
            inner = jnp.sum(unit * grad, axis=-1, keepdims=True)
            scaled = (grad - unit * inner) * over
            out[cut, :] = scaled * gain
            total = total + jnp.sum(hidden * scaled, axis=0, keepdims=True)
        return total

    gain_part = lax.fori_loop(0, rows // 16, finish, jnp.zeros((1, width), jnp.float32))

    for tile in range(width // 128):
        gain_out[tile : tile + 1, :] = gain_part[:, tile * 128 : (tile + 1) * 128]
    z, row = lax.rem(me, LINE), me // LINE
    plan = (
        (z, LINE, lambda i: (row * LINE + i, rep)),
        (row, n // LINE, lambda i: (i * LINE + z, rep)),
        (rep, reps, lambda i: (me, i)),
    )
    for turn, (here, size, target) in enumerate(plan):
        gain_slots[turn, here] = gain_out[...]

        def g_copy(off, slot):
            return pltpu.make_async_remote_copy(
                src_ref=gain_slots.at[turn, slot],
                dst_ref=gain_slots.at[turn, slot],
                send_sem=g_sems.at[turn, off],
                recv_sem=g_got.at[turn, slot],
                device_id=target(lax.rem(here + off, size)),
                device_id_type=MESH,
            )

        for off in range(1, size):
            g_copy(off, here).start()
        for off in range(1, size):
            g_copy(off, lax.rem(here + off, size)).wait_recv()
        total = gain_slots[turn, 0]
        for i in range(1, size):
            total = total + gain_slots[turn, i]
        gain_out[...] = total
        for off in range(1, size):
            g_copy(off, here).wait_send()

    all_others(idx_all, idx_sem, idx_got).wait_send()
    all_others(x_send, x_sem, idx_got).wait_send()
    all_others(t_send, t_sem, t_got).wait_send()
    all_others(shared, sh_sem, sh_got).wait_send()
    all_others(y_send, y_sem, y_got).wait_send()
    side.wait_send()
    for turn in range(1, STOPS):
        for copy in hop(turn):
            copy.wait_send()


def run(q_hidden, p_hidden, gain, idx):
    n, reps = lax.axis_size("batch"), lax.axis_size("rep")
    rows, width = q_hidden.shape
    places = n * SLOTS
    vmem = pl.BlockSpec(memory_space=pltpu.VMEM)
    bf16, f32 = jnp.bfloat16, jnp.float32
    dma = pltpu.SemaphoreType.DMA
    most = max(LINE, n // LINE, reps)
    return pl.pallas_call(
        functools.partial(kernel, n, reps),
        in_specs=[vmem] * 4,
        out_specs=[vmem] * 4,
        out_shape=[
            jax.ShapeDtypeStruct((rows, width), f32),
            jax.ShapeDtypeStruct((rows, width), f32),
            jax.ShapeDtypeStruct((1, rows), f32),
            jax.ShapeDtypeStruct((width // 128, 128), f32),
        ],
        scratch_shapes=[
            pltpu.VMEM((STOPS, rows, width), bf16),
            pltpu.VMEM((STOPS, rows, width), bf16),
            pltpu.VMEM((n, rows, 128), bf16),
            pltpu.VMEM((n, rows, 128), bf16),
            pltpu.VMEM((n, rows, 128), bf16),
            pltpu.VMEM((n, rows, 128), bf16),
            pltpu.VMEM((n, places, 128), bf16),
            pltpu.VMEM((n, places, 128), bf16),
            pltpu.VMEM((n, rows, 128), f32),
            pltpu.VMEM((n, 2 * SLOTS, 128), jnp.int32),
            pltpu.VMEM((places, 128), bf16),
            pltpu.VMEM((128, places), f32),
            pltpu.VMEM((n, 8, rows), f32),
            pltpu.VMEM((n, 8, rows), f32),
            pltpu.VMEM((n, 8, rows), f32),
            pltpu.VMEM((8, rows), f32),
            pltpu.VMEM((8, rows), f32),
            pltpu.VMEM((rows, 128), f32),
            pltpu.VMEM((rows, 128), f32),
            pltpu.VMEM((STOPS, rows, rows), bf16),
            pltpu.VMEM((STOPS, rows, rows), bf16),
            pltpu.VMEM((3, most, width // 128, 128), f32),
            dma,
            dma((n,)),
            dma,
            dma,
            dma,
            dma,
            dma,
            dma,
            dma,
            dma,
            dma((2, STOPS - 1)),
            dma((2, STOPS - 1)),
            dma,
            dma,
            dma((3, most)),
            dma((3, most)),
        ],
        compiler_params=pltpu.CompilerParams(
            collective_id=0, has_side_effects=True, vmem_limit_bytes=60 * MIB
        ),
        name="contrastive",
    )(q_hidden, p_hidden, gain.reshape(1, width), idx)


def slot_tables(wanted, peers):
    rows, neg = wanted.shape
    flat = wanted.T.reshape(-1)
    count = flat.shape[0]
    owner = flat // rows
    place = jnp.arange(count, dtype=jnp.int32)
    same = flat[:, None] == flat[None, :]
    again = jnp.any(same & (place[None, :] < place[:, None]), axis=1)
    smaller = (owner[:, None] == owner[None, :]) & (flat[:, None] < flat[None, :])
    rank = jnp.sum((smaller & ~again[:, None]).astype(jnp.int32), axis=0)
    slot = owner * SLOTS + rank
    key = rank * 128 + owner
    cells = jnp.arange(SLOTS * 128, dtype=jnp.int32)
    hit = (key[None, :] == cells[:, None]) & ~again[None, :]
    named = jnp.sum(jnp.where(hit, flat[None, :] % rows + 1, 0), axis=1) - 1
    pad = jnp.full((SLOTS - neg, rows), -1, jnp.int32)
    return jnp.concatenate([named.reshape(SLOTS, 128), slot.reshape(neg, rows), pad], axis=0)


def local(query_hidden, passage_hidden, norm_gain, negatives):
    idx = slot_tables(negatives[0], lax.axis_size("batch"))
    query_grad, passage_grad, loss, gain_grad = run(query_hidden[0], passage_hidden[0], norm_gain, idx)
    return (query_grad[None], passage_grad[None], loss, gain_grad.reshape(norm_gain.shape))


def solution(mesh):
    return jax.shard_map(
        local,
        mesh=mesh,
        in_specs=(P("rep", "batch", None), P("rep", "batch", None), P(), P("rep", "batch", None)),
        out_specs=(P("rep", "batch", None), P("rep", "batch", None), P("rep", "batch"), P()),
        check_vma=False,
    )
```

```python
import functools

import jax
import jax.numpy as jnp
from jax import lax
from jax.experimental import pallas as pl
from jax.experimental.pallas import tpu as pltpu
from jax.sharding import PartitionSpec as P

STOPS = 4
TEMP = 0.05
EPS = 1e-06
SLOTS = 8
LINE = 8
STRIDE, UNSTRIDE = 27, 19
FIRST_HOP = (22, 27)
SECOND_HOP = (20, 50)
MIB = 1 << 20
MESH = pl.DeviceIdType.MESH
NT = (((1,), (1,)), ((), ()))
TN = (((0,), (0,)), ((), ()))


def dot(a, b, dims=(((1,), (0,)), ((), ()))):
    return lax.dot_general(a, b, dims, preferred_element_type=jnp.float32)


def kernel(
    n, reps, q_hbm, p_hbm, gain_ref, idx_ref, q_out, p_out, loss_ref, gain_out,
    q_ref, p_ref, q_acc, p_acc, p_win, q_win, x_send, w, yq_send, yq_recv, yp_send, yp_recv, table, sums,
    idx_all, asks, asks_t, t_send, t_recv, shared, side_send, side_recv, q_norm, p_norm, q_weight, p_weight,
    gain_part, gain_near, gain_far, gain_all,
    in_sems, out_sems, x_sem, x_sems, idx_sem, idx_got, t_sem, t_got, sh_sem, sh_sems, yq_sem, yq_got, yp_sem, yp_got,
    chain_sem, chain_got, side_sem, side_got, g_sems, g_got,
):
    me, rep = lax.axis_index("batch"), lax.axis_index("rep")
    rows, width = q_ref.shape
    half = rows // 2
    neg = 3
    places = n * SLOTS
    tiles = width // 128

    def ahead(i):
        return lax.rem(me + STRIDE * i, n)

    def behind(i):
        return lax.rem(me + n * STRIDE - STRIDE * i, n)

    def position(device):
        return lax.rem((me + n - device) * UNSTRIDE, n)

    def remote(src, dst, send, recv, device, group=rep):
        return pltpu.make_async_remote_copy(
            src_ref=src, dst_ref=dst, send_sem=send, recv_sem=recv, device_id=(device, group), device_id_type=MESH
        )

    inputs = (pltpu.make_async_copy(q_hbm, q_ref, in_sems.at[0]), pltpu.make_async_copy(p_hbm, p_ref, in_sems.at[1]))
    for copy in inputs:
        copy.start()

    barrier = pltpu.get_barrier_semaphore()
    z, row = lax.rem(me, LINE), me // LINE
    lines = n // LINE

    def greet(i, carry):
        pl.semaphore_signal(barrier, inc=1, device_id=(ahead(i), rep), device_id_type=MESH)
        return carry

    def greet_group(i, carry):
        group = lax.rem(rep + 1 + i // lines, reps)
        device = lax.rem(i, lines) * LINE + z
        pl.semaphore_signal(barrier, inc=1, device_id=(device, group), device_id_type=MESH)
        return carry

    lax.fori_loop(1, n, greet, 0)
    lax.fori_loop(0, (reps - 1) * lines, greet_group, 0)
    for copy in inputs:
        copy.wait()

    def normalize(chunk, carry):
        cut = pl.ds(pl.multiple_of(chunk * 16, 16), 16)
        units = []
        for src, win, norm in ((q_ref, q_win, q_norm), (p_ref, p_win, p_norm)):
            scaled = src[cut, :].astype(jnp.float32) * gain_ref[...]
            length = jnp.sqrt(jnp.sum(scaled * scaled, axis=-1, keepdims=True) + EPS)
            unit = scaled * (1.0 / length)
            win[0, cut, :] = unit.astype(jnp.bfloat16)
            norm[cut, :] = jnp.broadcast_to(1.0 / length, (16, 128))
            units.append(unit)
        low = lax.broadcasted_iota(jnp.int32, (16, 128), 1) < 64
        for tile in range(tiles):
            q_tile = units[0][:, tile * 128 : (tile + 1) * 128]
            p_tile = units[1][:, tile * 128 : (tile + 1) * 128]
            x_send[2 * tile, cut, :] = jnp.where(low, q_tile, pltpu.roll(p_tile, 64, 1)).astype(jnp.bfloat16)
            x_send[2 * tile + 1, cut, :] = jnp.where(low, pltpu.roll(q_tile, 64, 1), p_tile).astype(jnp.bfloat16)
        return carry

    lax.fori_loop(0, rows // 16, normalize, 0)
    w[0] = x_send[me]
    pl.semaphore_wait(barrier, n - 1 + (reps - 1) * lines)

    def x_copy(i):
        return remote(x_send.at[ahead(i)], w.at[i], x_sem, x_sems.at[i], ahead(i))

    def start_x(i, carry):
        x_copy(i).start()
        return carry

    lax.fori_loop(1, n, start_x, 0)

    flat = idx_ref[...]
    flat_f = flat.astype(jnp.float32)
    owner_row = (flat >> 7).astype(jnp.float32)
    columns = jnp.concatenate([flat_f, jnp.zeros((rows - neg, rows), jnp.float32)], axis=0).T
    owner_columns = (columns.astype(jnp.int32) >> 7).astype(jnp.float32)
    down = lax.broadcasted_iota(jnp.int32, (rows, rows), 0)
    across = lax.broadcasted_iota(jnp.int32, (rows, rows), 1)
    again_row, again_column, ranks = [], [], []
    for k in range(neg):
        seen = jnp.zeros((rows, rows), jnp.float32)
        seen_t = jnp.zeros((rows, rows), jnp.float32)
        for j in range(k + 1):
            same = columns[:, j : j + 1] == flat_f[k : k + 1]
            same_t = columns[:, k : k + 1] == flat_f[j : j + 1]
            if j == k:
                same, same_t = same & (down < across), same_t & (across < down)
            seen = seen + jnp.where(same, 1.0, 0.0)
            seen_t = seen_t + jnp.where(same_t, 1.0, 0.0)
        again_row.append(jnp.sum(seen, axis=0, keepdims=True))
        again_column.append(jnp.sum(seen_t, axis=1, keepdims=True))
    for k in range(neg):
        count = jnp.zeros((rows, rows), jnp.float32)
        for j in range(neg):
            lower = (owner_columns[:, j : j + 1] == owner_row[k : k + 1]) & (columns[:, j : j + 1] < flat_f[k : k + 1])
            count = count + jnp.where(lower & (again_column[j] == 0.0), 1.0, 0.0)
        ranks.append(jnp.sum(count, axis=0, keepdims=True))
    named = jnp.zeros((SLOTS, 128), jnp.float32)
    at_rank = lax.broadcasted_iota(jnp.int32, (SLOTS, rows), 0).astype(jnp.float32)
    for k in range(neg):
        first = (at_rank == ranks[k]) & (again_row[k] == 0.0)
        value = jnp.where(first, (flat[k : k + 1] & 127).astype(jnp.float32) + 1.0, 0.0).astype(jnp.bfloat16)
        at_owner = jnp.where(owner_columns[:, k : k + 1] == across.astype(jnp.float32), 1.0, 0.0).astype(jnp.bfloat16)
        named = named + dot(value, at_owner)
    lines_of = [named - 1.0, owner_row] + ranks + [jnp.zeros((2, 128), jnp.float32)]
    idx_all[0] = jnp.concatenate(lines_of, axis=0).astype(jnp.bfloat16)
    own_entry = flat == me * rows + lax.broadcasted_iota(jnp.int32, flat.shape, 1)

    def start_idx(i, carry):
        remote(idx_all.at[0], idx_all.at[i], idx_sem, idx_got, ahead(i)).start()
        return carry

    lax.fori_loop(1, n, start_idx, 0)

    right, left = lax.rem(me + 1, n), lax.rem(me + n - 1, n)

    def hop(turn, part):
        cut = pl.ds(part * half, half)
        sems = [(chain_sem.at[way, turn - 1, part], chain_got.at[way, turn - 1, part]) for way in range(2)]
        return (
            remote(p_win.at[turn - 1, cut], p_win.at[turn, cut], *sems[0], right),
            remote(q_win.at[turn - 1, cut], q_win.at[turn, cut], *sems[1], left),
        )

    def start_hop(turn, part):
        for copy in hop(turn, part):
            copy.start()

    def pass_on(turn, part):
        for copy in hop(turn, part):
            copy.wait_recv()
        if turn + 1 < STOPS:
            start_hop(turn + 1, part)

    others = pl.ds(1, n - 1)

    def all_others(buffer, send, recv):
        return remote(buffer.at[others], buffer.at[others], send, recv, right)

    all_others(idx_all, idx_sem, idx_got).wait_recv()
    wide = idx_all[...].astype(jnp.float32)[:, :SLOTS, :].reshape(places, 128)
    asks[...] = wide.astype(jnp.bfloat16)
    asks_t[...] = wide.T

    def pick(step, carry):
        for part in range(2):

            @pl.when(step == FIRST_HOP[part] * n // 64)
            def _():
                start_hop(1, part)

        picked = []
        for part in range(2):
            pos = 2 * step + part

            @pl.when(pos > 0)
            def _():
                x_copy(pos).wait_recv()

            owner = behind(pos)
            column = (lax.broadcasted_iota(jnp.int32, (128, 128), 0) == owner).astype(jnp.bfloat16)
            asked = dot(asks[...], column)
            lane = lax.broadcasted_iota(jnp.int32, asked.shape, 1).astype(jnp.float32)
            hot = jnp.where(asked == lane, 1.0, 0.0).astype(jnp.bfloat16)
            picked.append(dot(hot, w[pos]).reshape(n, SLOTS, 128))
        both = jnp.concatenate(picked, axis=1).astype(jnp.bfloat16)
        table[:, pl.ds(pl.multiple_of(step * 16, 16), 16), :] = both
        return carry

    lax.fori_loop(0, n // 2, pick, 0)

    def places_of(pos):
        entry = idx_all[pos].astype(jnp.float32).astype(jnp.int32)
        owner, rank = entry[SLOTS : SLOTS + neg], entry[SLOTS + neg : SLOTS + 2 * neg]
        return (((me + n - owner) * UNSTRIDE) & (n - 1)) * SLOTS + rank

    def t_copy(pos):
        return remote(t_send.at[pos], t_recv.at[n - pos], t_sem, t_got, behind(pos))

    def partial_scores(pos):
        mine = w[pos].astype(jnp.float32)
        lane = lax.broadcasted_iota(jnp.int32, mine.shape, 1)
        query = jnp.where(lane < 64, 0.0, pltpu.roll(mine, 64, 1)).astype(jnp.bfloat16)
        scores = dot(table[pos], query, NT)
        place = lax.broadcasted_iota(jnp.int32, scores.shape, 0)
        slot = places_of(pos)
        parts = [
            jnp.sum(jnp.where(place == slot[k : k + 1], scores, 0.0), axis=0, keepdims=True) for k in range(neg)
        ]
        return jnp.concatenate(parts + [jnp.zeros((8 - neg, rows), jnp.float32)], axis=0)

    def score_step(pos, carry):
        for part in range(2):

            @pl.when(pos == SECOND_HOP[part] * n // 64)
            def _():
                pass_on(1, part)

        t_send[pos] = partial_scores(pos)
        t_copy(pos).start()
        return carry

    lax.fori_loop(1, n, score_step, 0)
    t_recv[0] = partial_scores(0)

    def window_scores(p_slot, q_slot, p_rows=(0, rows), q_count=1):
        step = 512

        def add(tile, total):
            cut = pl.ds(pl.multiple_of(tile * step, step), step)
            down_block = p_win[p_slot, p_rows[0] : p_rows[0] + p_rows[1], cut]
            across_block = q_win[q_slot : q_slot + q_count, :, cut].reshape(q_count * rows, step)
            return total + dot(down_block, across_block, NT)

        start = jnp.zeros((p_rows[1], q_count * rows), jnp.float32)
        return lax.fori_loop(0, width // step, add, start) / TEMP

    own = window_scores(0, 0)
    eye = down == across
    positive = jnp.sum(jnp.where(eye, own, 0.0), axis=0, keepdims=True)
    exps = [jnp.exp(own), jnp.exp(window_scores(1, 0))]
    pass_on(2, 0)
    upper = jnp.exp(window_scores(2, 0, (0, half), 2))
    pass_on(2, 1)
    lower = jnp.exp(window_scores(2, 0, (half, half), 2))
    far = jnp.sum(upper[:, rows:], axis=0, keepdims=True) + jnp.sum(lower[:, rows:], axis=0, keepdims=True)
    side_send[...] = jnp.broadcast_to(far, side_send.shape)
    side = remote(side_send, side_recv, side_sem, side_got, right)
    side.start()
    exps.append(jnp.concatenate([upper[:, :rows], lower[:, :rows]], axis=0))
    near = sum(jnp.sum(e, axis=0, keepdims=True) for e in exps)

    all_others(t_recv, t_sem, t_got).wait_recv()
    t = lax.fori_loop(0, n, lambda i, total: total + t_recv[i], jnp.zeros((8, rows), jnp.float32)) / TEMP
    exp_t = jnp.exp(t)
    side.wait_recv()
    partition = near + side_recv[:1] + sum(exp_t[k : k + 1] for k in range(neg))
    inverse = 1.0 / partition
    v = (exp_t[:neg] * inverse).astype(jnp.bfloat16).astype(jnp.float32)
    own_v = jnp.sum(jnp.where(own_entry, v, 0.0), axis=0, keepdims=True)
    v = jnp.where(own_entry, -v, v)
    shared[0] = jnp.concatenate([v, jnp.broadcast_to(inverse, (8 - neg, rows))], axis=0)

    def sh_copy(i):
        return remote(shared.at[0], shared.at[i], sh_sem, sh_sems.at[i], ahead(i))

    def start_sh(i, carry):
        sh_copy(i).start()
        return carry

    lax.fori_loop(1, n, start_sh, 0)
    loss_ref[...] = jnp.log(partition) - positive
    for stop in range(STOPS - 1):
        weight = exps[stop] * inverse
        if stop == 0:
            weight = (weight - jnp.where(eye, 1.0, 0.0)).astype(jnp.bfloat16).astype(jnp.float32)
            p_weight[0] = weight.astype(jnp.bfloat16)
            weight = weight + jnp.where(eye, own_v, 0.0)
        q_weight[stop] = weight.T.astype(jnp.bfloat16)

    def yq_copy(pos):
        return remote(yq_send.at[pos], yq_recv.at[n - pos], yq_sem, yq_got, behind(pos))

    def fold(block, lanes):
        first, second = block[:half], block[half:]
        low = lax.broadcasted_iota(jnp.int32, (half, 128), 1) < 64
        if lanes == 0:
            return jnp.where(low, first, pltpu.roll(second, 64, 1)).astype(jnp.bfloat16)
        return jnp.where(low, pltpu.roll(first, 64, 1), second).astype(jnp.bfloat16)

    def spread(step, carry):
        grads = []
        for part in range(2):
            pos = 2 * step + part

            @pl.when(pos > 0)
            def _():
                sh_copy(pos).wait_recv()

            place = lax.broadcasted_iota(jnp.int32, (places, rows), 0)
            slot = places_of(pos)
            weight = jnp.zeros((places, rows), jnp.float32)
            for k in range(neg):
                weight = weight + jnp.where(place == slot[k : k + 1], shared[pos, k : k + 1, :], 0.0)
            q_side = jnp.maximum(weight, 0.0).astype(jnp.bfloat16)
            p_side = jnp.abs(weight).astype(jnp.bfloat16)
            yq_send[pos] = fold(dot(q_side, table[pos], TN) / TEMP, 64)

            @pl.when(pos > 0)
            def _():
                yq_copy(pos).start()

            grads.append((dot(p_side, w[pos]) / TEMP).reshape(n, SLOTS, 128))
        both = jnp.concatenate(grads, axis=1).astype(jnp.bfloat16)
        sums[:, pl.ds(pl.multiple_of(step * 16, 16), 16), :] = both
        return carry

    lax.fori_loop(0, n // 2, spread, 0)
    yq_recv[0] = yq_send[0]

    def yp_copy(pos):
        return remote(yp_send.at[pos], yp_recv.at[n - pos], yp_sem, yp_got, behind(pos))

    def gather_tile(pos):
        asked = asks_t[pl.ds(behind(pos), 1), :]
        target = lax.broadcasted_iota(jnp.int32, (rows, places), 0).astype(jnp.float32)
        hot = jnp.where(target == asked, 1.0, 0.0).astype(jnp.bfloat16)
        return fold(dot(hot, sums[pos]), 0)

    def gather_step(pos, carry):
        yp_send[pos] = gather_tile(pos)
        yp_copy(pos).start()
        return carry

    lax.fori_loop(1, n, gather_step, 0)
    yp_recv[0] = gather_tile(0)

    pass_on(3, 0)
    pass_on(3, 1)

    def inverse_of(stop):
        return shared[position(lax.rem(me + stop, n)), neg : neg + 1, :]

    for stop in range(1, STOPS):
        p_weight[stop] = (jnp.exp(window_scores(0, stop)) * inverse_of(stop)).astype(jnp.bfloat16)
    q_weight[STOPS - 1] = (jnp.exp(window_scores(STOPS - 1, 0)) * inverse).T.astype(jnp.bfloat16)

    def products(tile, carry):
        cut = pl.ds(pl.multiple_of(tile * 256, 256), 256)
        q_grad = jnp.zeros((rows, 256), jnp.float32)
        p_grad = jnp.zeros((rows, 256), jnp.float32)
        for stop in range(STOPS):
            q_grad = q_grad + dot(q_weight[stop], p_win[stop, :, cut])
            p_grad = p_grad + dot(p_weight[stop], q_win[stop, :, cut])
        q_acc[:, cut] = q_grad / TEMP
        p_acc[:, cut] = p_grad / TEMP
        return carry

    lax.fori_loop(0, width // 256, products, 0)

    all_others(yq_recv, yq_sem, yq_got).wait_recv()
    all_others(yp_recv, yp_sem, yp_got).wait_recv()

    def finish(chunk, total):
        cut = pl.ds(pl.multiple_of(chunk * 16, 16), 16)
        upper_cut = pl.ds(pl.multiple_of(half + chunk * 16, 16), 16)
        low = lax.broadcasted_iota(jnp.int32, (16, 128), 1) < 64
        for src, norm, recv, out in ((q_ref, q_norm, yq_recv, q_acc), (p_ref, p_norm, yp_recv, p_acc)):
            for tile in range(tiles):
                lanes = slice(tile * 128, (tile + 1) * 128)
                even = recv[position(2 * tile), cut, :].astype(jnp.float32)
                odd = recv[position(2 * tile + 1), cut, :].astype(jnp.float32)
                out[cut, lanes] += jnp.where(low, even, pltpu.roll(odd, 64, 1))
                out[upper_cut, lanes] += jnp.where(low, pltpu.roll(even, 64, 1), odd)
            for here in (cut, upper_cut):
                hidden = src[here, :].astype(jnp.float32)
                over = norm[here, :1]
                gain = gain_ref[...]
                unit = hidden * gain * over
                grad = out[here, :]
                inner = jnp.sum(unit * grad, axis=-1, keepdims=True)
                scaled = (grad - unit * inner) * over
                out[here, :] = scaled * gain
                each = hidden * scaled
                total = total + each[:8] + each[8:]
        return total

    total = lax.fori_loop(0, half // 16, finish, jnp.zeros((8, width), jnp.float32))

    total = jnp.sum(total, axis=0, keepdims=True)
    each = max(1, tiles // LINE)
    gain_part[...] = jnp.zeros_like(gain_part)
    for tile in range(tiles):
        gain_part[tile // each, tile % each : tile % each + 1, :] = total[:, tile * 128 : (tile + 1) * 128]
    outputs = (pltpu.make_async_copy(q_acc, q_out, out_sems.at[0]), pltpu.make_async_copy(p_acc, p_out, out_sems.at[1]))

    def near_copy(off):
        to = lax.rem(z + off, LINE)
        return remote(gain_part.at[to], gain_near.at[off], g_sems.at[0], g_got.at[0], row * LINE + to)

    size = lines * reps
    spot = row * reps + rep

    def far_copy(off):
        to = lax.rem(spot + off, size)
        return remote(
            gain_far.at[0], gain_far.at[off], g_sems.at[1], g_got.at[1], to // reps * LINE + z, lax.rem(to, reps)
        )

    def all_copy(off):
        to = lax.rem(z + off, LINE)
        return remote(gain_all.at[0], gain_all.at[off], g_sems.at[2], g_got.at[2], row * LINE + to)

    def whole(buffer, turn):
        cut = pl.ds(1, buffer.shape[0] - 1)
        return remote(buffer.at[cut], buffer.at[cut], g_sems.at[turn], g_got.at[turn], right)

    for off in range(1, LINE):
        near_copy(off).start()
    for copy in outputs:
        copy.start()
    whole(gain_near, 0).wait_recv()
    piece = gain_part[z]
    for off in range(1, LINE):
        piece = piece + gain_near[off]
    gain_far[0] = piece

    def start_far(off, carry):
        far_copy(off).start()
        return carry

    lax.fori_loop(1, size, start_far, 0)
    whole(gain_far, 1).wait_recv()
    gain_all[0] = lax.fori_loop(
        0, size, lambda i, add: add + gain_far[lax.rem(spot + size - i, size)], jnp.zeros((8, 128), jnp.float32)
    )
    for off in range(1, LINE):
        all_copy(off).start()
    whole(gain_all, 2).wait_recv()
    for tile in range(tiles):
        gain_out[tile : tile + 1, :] = gain_all[lax.rem(z + LINE - tile // each, LINE), tile % each : tile % each + 1, :]

    all_others(idx_all, idx_sem, idx_got).wait_send()
    all_others(x_send, x_sem, idx_got).wait_send()
    all_others(t_send, t_sem, t_got).wait_send()
    all_others(shared, sh_sem, idx_got).wait_send()
    all_others(yq_send, yq_sem, yq_got).wait_send()
    all_others(yp_send, yp_sem, yp_got).wait_send()
    side.wait_send()
    for turn in range(1, STOPS):
        for part in range(2):
            for copy in hop(turn, part):
                copy.wait_send()
    for turn, buffer in enumerate((gain_near, gain_far, gain_all)):
        whole(buffer, turn).wait_send()
    for copy in outputs:
        copy.wait()


def run(q_hidden, p_hidden, gain, idx):
    n, reps = lax.axis_size("batch"), lax.axis_size("rep")
    rows, width = q_hidden.shape
    half = rows // 2
    places = n * SLOTS
    vmem, hbm = pl.BlockSpec(memory_space=pltpu.VMEM), pl.BlockSpec(memory_space=pl.ANY)
    bf16, f32 = jnp.bfloat16, jnp.float32
    dma = pltpu.SemaphoreType.DMA
    return pl.pallas_call(
        functools.partial(kernel, n, reps),
        in_specs=[hbm, hbm, vmem, vmem],
        out_specs=[hbm, hbm, vmem, vmem],
        out_shape=[
            jax.ShapeDtypeStruct((rows, width), f32),
            jax.ShapeDtypeStruct((rows, width), f32),
            jax.ShapeDtypeStruct((1, rows), f32),
            jax.ShapeDtypeStruct((width // 128, 128), f32),
        ],
        scratch_shapes=[
            pltpu.VMEM((rows, width), bf16),
            pltpu.VMEM((rows, width), bf16),
            pltpu.VMEM((rows, width), f32),
            pltpu.VMEM((rows, width), f32),
            pltpu.VMEM((STOPS, rows, width), bf16),
            pltpu.VMEM((STOPS, rows, width), bf16),
            pltpu.VMEM((n, rows, 128), bf16),
            pltpu.VMEM((n, rows, 128), bf16),
            pltpu.VMEM((n, half, 128), bf16),
            pltpu.VMEM((n, half, 128), bf16),
            pltpu.VMEM((n, half, 128), bf16),
            pltpu.VMEM((n, half, 128), bf16),
            pltpu.VMEM((n, places, 128), bf16),
            pltpu.VMEM((n, places, 128), bf16),
            pltpu.VMEM((n, 2 * SLOTS, 128), bf16),
            pltpu.VMEM((places, 128), bf16),
            pltpu.VMEM((128, places), f32),
            pltpu.VMEM((n, 8, rows), f32),
            pltpu.VMEM((n, 8, rows), f32),
            pltpu.VMEM((n, 8, rows), f32),
            pltpu.VMEM((8, rows), f32),
            pltpu.VMEM((8, rows), f32),
            pltpu.VMEM((rows, 128), f32),
            pltpu.VMEM((rows, 128), f32),
            pltpu.VMEM((STOPS, rows, rows), bf16),
            pltpu.VMEM((STOPS, rows, rows), bf16),
            pltpu.VMEM((LINE, 8, 128), f32),
            pltpu.VMEM((LINE, 8, 128), f32),
            pltpu.VMEM((n // LINE * reps, 8, 128), f32),
            pltpu.VMEM((LINE, 8, 128), f32),
            dma((2,)),
            dma((2,)),
            dma,
            dma((n,)),
            dma,
            dma,
            dma,
            dma,
            dma,
            dma((n,)),
            dma,
            dma,
            dma,
            dma,
            dma((2, STOPS - 1, 2)),
            dma((2, STOPS - 1, 2)),
            dma,
            dma,
            dma((3,)),
            dma((3,)),
        ],
        compiler_params=pltpu.CompilerParams(
            collective_id=0, has_side_effects=True, vmem_limit_bytes=60 * MIB
        ),
        name="contrastive",
    )(q_hidden, p_hidden, gain.reshape(1, width), idx)


def local(query_hidden, passage_hidden, norm_gain, negatives):
    query_grad, passage_grad, loss, gain_grad = run(query_hidden[0], passage_hidden[0], norm_gain, negatives[0].T)
    return (query_grad[None], passage_grad[None], loss, gain_grad.reshape(norm_gain.shape))


def solution(mesh):
    return jax.shard_map(
        local,
        mesh=mesh,
        in_specs=(P("rep", "batch", None), P("rep", "batch", None), P(), P("rep", "batch", None)),
        out_specs=(P("rep", "batch", None), P("rep", "batch", None), P("rep", "batch"), P()),
        check_vma=False,
    )
```

```python
import functools

import jax
import jax.numpy as jnp
from jax import lax
from jax.experimental import pallas as pl
from jax.experimental.pallas import tpu as pltpu
from jax.sharding import PartitionSpec as P

STOPS = 4
TEMP = 0.05
EPS = 1e-06
SLOTS = 8
LINE = 8
STRIDE, UNSTRIDE = 27, 19
PARTS = 4
SECOND_HOP = (6, 20, 34, 48)
MIB = 1 << 20
MESH = pl.DeviceIdType.MESH
NT = (((1,), (1,)), ((), ()))
TN = (((0,), (0,)), ((), ()))


def dot(a, b, dims=(((1,), (0,)), ((), ()))):
    return lax.dot_general(a, b, dims, preferred_element_type=jnp.float32)


def kernel(
    n, reps, q_hbm, p_hbm, gain_ref, idx_ref, q_out, p_out, loss_ref, gain_out,
    q_ref, p_ref, q_acc, p_acc, p_win, q_win, x_send, w, y_send, y_recv, table, sums, q_part,
    idx_all, asks, asks_t, t_send, t_recv, shared, side_send, side_recv, q_norm, p_norm, q_weight, p_weight,
    gain_part, gain_near, gain_far, gain_all,
    in_sems, out_sems, x_sem, x_sems, idx_sem, idx_got, t_sem, t_got, sh_sem, sh_sems, y_sem, y_got,
    chain_sem, chain_got, side_sem, side_got, g_sems, g_got,
):
    me, rep = lax.axis_index("batch"), lax.axis_index("rep")
    rows, width = q_ref.shape
    half, quarter = rows // 2, rows // PARTS
    neg = 3
    places = n * SLOTS
    tiles = width // 128

    def ahead(i):
        return lax.rem(me + STRIDE * i, n)

    def behind(i):
        return lax.rem(me + n * STRIDE - STRIDE * i, n)

    def position(device):
        return lax.rem((me + n - device) * UNSTRIDE, n)

    def remote(src, dst, send, recv, device, group=rep):
        return pltpu.make_async_remote_copy(
            src_ref=src, dst_ref=dst, send_sem=send, recv_sem=recv, device_id=(device, group), device_id_type=MESH
        )

    inputs = (pltpu.make_async_copy(q_hbm, q_ref, in_sems.at[0]), pltpu.make_async_copy(p_hbm, p_ref, in_sems.at[1]))
    for copy in inputs:
        copy.start()

    barrier = pltpu.get_barrier_semaphore()
    z, row = lax.rem(me, LINE), me // LINE
    lines = n // LINE

    def greet(i, carry):
        pl.semaphore_signal(barrier, inc=1, device_id=(ahead(i), rep), device_id_type=MESH)
        return carry

    def greet_group(i, carry):
        group = lax.rem(rep + 1 + i // lines, reps)
        device = lax.rem(i, lines) * LINE + z
        pl.semaphore_signal(barrier, inc=1, device_id=(device, group), device_id_type=MESH)
        return carry

    lax.fori_loop(1, n, greet, 0)
    lax.fori_loop(0, (reps - 1) * lines, greet_group, 0)

    flat = idx_ref[...]
    flat_f = flat.astype(jnp.float32)
    owner_row = (flat >> 7).astype(jnp.float32)
    columns = jnp.concatenate([flat_f, jnp.zeros((rows - neg, rows), jnp.float32)], axis=0).T
    owner_columns = (columns.astype(jnp.int32) >> 7).astype(jnp.float32)
    down = lax.broadcasted_iota(jnp.int32, (rows, rows), 0)
    across = lax.broadcasted_iota(jnp.int32, (rows, rows), 1)
    again_row, again_column, ranks = [], [], []
    for k in range(neg):
        seen = jnp.zeros((rows, rows), jnp.float32)
        seen_t = jnp.zeros((rows, rows), jnp.float32)
        for j in range(k + 1):
            same = columns[:, j : j + 1] == flat_f[k : k + 1]
            same_t = columns[:, k : k + 1] == flat_f[j : j + 1]
            if j == k:
                same, same_t = same & (down < across), same_t & (across < down)
            seen = seen + jnp.where(same, 1.0, 0.0)
            seen_t = seen_t + jnp.where(same_t, 1.0, 0.0)
        again_row.append(jnp.sum(seen, axis=0, keepdims=True))
        again_column.append(jnp.sum(seen_t, axis=1, keepdims=True))
    for k in range(neg):
        count = jnp.zeros((rows, rows), jnp.float32)
        for j in range(neg):
            lower = (owner_columns[:, j : j + 1] == owner_row[k : k + 1]) & (columns[:, j : j + 1] < flat_f[k : k + 1])
            count = count + jnp.where(lower & (again_column[j] == 0.0), 1.0, 0.0)
        ranks.append(jnp.sum(count, axis=0, keepdims=True))
    named = jnp.zeros((SLOTS, 128), jnp.float32)
    at_rank = lax.broadcasted_iota(jnp.int32, (SLOTS, rows), 0).astype(jnp.float32)
    for k in range(neg):
        first = (at_rank == ranks[k]) & (again_row[k] == 0.0)
        value = jnp.where(first, (flat[k : k + 1] & 127).astype(jnp.float32) + 1.0, 0.0).astype(jnp.bfloat16)
        at_owner = jnp.where(owner_columns[:, k : k + 1] == across.astype(jnp.float32), 1.0, 0.0).astype(jnp.bfloat16)
        named = named + dot(value, at_owner)
    lines_of = [named - 1.0, owner_row] + ranks + [jnp.zeros((2, 128), jnp.float32)]
    idx_all[0] = jnp.concatenate(lines_of, axis=0).astype(jnp.bfloat16)
    own_entry = flat == me * rows + lax.broadcasted_iota(jnp.int32, flat.shape, 1)

    for copy in inputs:
        copy.wait()

    def normalize(chunk, carry):
        cut = pl.ds(pl.multiple_of(chunk * 16, 16), 16)
        units = []
        for src, win, norm in ((q_ref, q_win, q_norm), (p_ref, p_win, p_norm)):
            scaled = src[cut, :].astype(jnp.float32) * gain_ref[...]
            length = jnp.sqrt(jnp.sum(scaled * scaled, axis=-1, keepdims=True) + EPS)
            unit = scaled * (1.0 / length)
            win[0, cut, :] = unit.astype(jnp.bfloat16)
            norm[cut, :] = jnp.broadcast_to(1.0 / length, (16, 128))
            units.append(unit)
        low = lax.broadcasted_iota(jnp.int32, (16, 128), 1) < 64
        for tile in range(tiles):
            q_tile = units[0][:, tile * 128 : (tile + 1) * 128]
            p_tile = units[1][:, tile * 128 : (tile + 1) * 128]
            x_send[2 * tile, cut, :] = jnp.where(low, q_tile, pltpu.roll(p_tile, 64, 1)).astype(jnp.bfloat16)
            x_send[2 * tile + 1, cut, :] = jnp.where(low, pltpu.roll(q_tile, 64, 1), p_tile).astype(jnp.bfloat16)
        return carry

    lax.fori_loop(0, rows // 16, normalize, 0)
    w[0] = x_send[me]
    pl.semaphore_wait(barrier, n - 1 + (reps - 1) * lines)

    def start_idx(i, carry):
        remote(idx_all.at[0], idx_all.at[i], idx_sem, idx_got, ahead(i)).start()
        return carry

    lax.fori_loop(1, n, start_idx, 0)

    def x_copy(i):
        return remote(x_send.at[ahead(i)], w.at[i], x_sem, x_sems.at[i], ahead(i))

    def start_x(i, carry):
        x_copy(i).start()
        return carry

    lax.fori_loop(1, n, start_x, 0)

    right, left = lax.rem(me + 1, n), lax.rem(me + n - 1, n)

    def hop(turn, part):
        cut = pl.ds(part * quarter, quarter)
        sems = [(chain_sem.at[way, turn - 1, part], chain_got.at[way, turn - 1, part]) for way in range(2)]
        return (
            remote(p_win.at[turn - 1, cut], p_win.at[turn, cut], *sems[0], right),
            remote(q_win.at[turn - 1, cut], q_win.at[turn, cut], *sems[1], left),
        )

    def start_hop(turn, part):
        for copy in hop(turn, part):
            copy.start()

    def pass_on(turn, part):
        for copy in hop(turn, part):
            copy.wait_recv()
        if turn + 1 < STOPS:
            start_hop(turn + 1, part)

    for part in range(PARTS):
        start_hop(1, part)

    others = pl.ds(1, n - 1)

    def all_others(buffer, send, recv):
        return remote(buffer.at[others], buffer.at[others], send, recv, right)

    all_others(idx_all, idx_sem, idx_got).wait_recv()
    wide = idx_all[...].astype(jnp.float32)[:, :SLOTS, :].reshape(places, 128)
    asks[...] = wide.astype(jnp.bfloat16)
    asks_t[...] = wide.T

    def pick(step, carry):
        picked = []
        for part in range(2):
            pos = 2 * step + part

            @pl.when(pos > 0)
            def _():
                x_copy(pos).wait_recv()

            owner = behind(pos)
            column = (lax.broadcasted_iota(jnp.int32, (128, 128), 0) == owner).astype(jnp.bfloat16)
            asked = dot(asks[...], column)
            lane = lax.broadcasted_iota(jnp.int32, asked.shape, 1).astype(jnp.float32)
            hot = jnp.where(asked == lane, 1.0, 0.0).astype(jnp.bfloat16)
            picked.append(dot(hot, w[pos]).reshape(n, SLOTS, 128))
        both = jnp.concatenate(picked, axis=1).astype(jnp.bfloat16)
        table[:, pl.ds(pl.multiple_of(step * 16, 16), 16), :] = both
        return carry

    lax.fori_loop(0, n // 2, pick, 0)

    def places_of(pos):
        entry = idx_all[pos].astype(jnp.float32).astype(jnp.int32)
        owner, rank = entry[SLOTS : SLOTS + neg], entry[SLOTS + neg : SLOTS + 2 * neg]
        return (((me + n - owner) * UNSTRIDE) & (n - 1)) * SLOTS + rank

    def t_copy(pos):
        return remote(t_send.at[pos], t_recv.at[n - pos], t_sem, t_got, behind(pos))

    def partial_scores(pos):
        mine = w[pos].astype(jnp.float32)
        lane = lax.broadcasted_iota(jnp.int32, mine.shape, 1)
        query = jnp.where(lane < 64, 0.0, pltpu.roll(mine, 64, 1)).astype(jnp.bfloat16)
        scores = dot(table[pos], query, NT)
        place = lax.broadcasted_iota(jnp.int32, scores.shape, 0)
        slot = places_of(pos)
        parts = [
            jnp.sum(jnp.where(place == slot[k : k + 1], scores, 0.0), axis=0, keepdims=True) for k in range(neg)
        ]
        return jnp.concatenate(parts + [jnp.zeros((8 - neg, rows), jnp.float32)], axis=0)

    def score_step(pos, carry):
        for part in range(PARTS):

            @pl.when(pos == max(1, SECOND_HOP[part] * n // 64))
            def _():
                pass_on(1, part)

        t_send[pos] = partial_scores(pos)
        t_copy(pos).start()
        return carry

    lax.fori_loop(1, n, score_step, 0)
    t_recv[0] = partial_scores(0)

    def window_scores(p_slot, q_slot, p_rows=(0, rows), q_count=1):
        step = 512

        def add(tile, total):
            cut = pl.ds(pl.multiple_of(tile * step, step), step)
            down_block = p_win[p_slot, p_rows[0] : p_rows[0] + p_rows[1], cut]
            across_block = q_win[q_slot : q_slot + q_count, :, cut].reshape(q_count * rows, step)
            return total + dot(down_block, across_block, NT)

        start = jnp.zeros((p_rows[1], q_count * rows), jnp.float32)
        return lax.fori_loop(0, width // step, add, start) / TEMP

    own = window_scores(0, 0)
    eye = down == across
    positive = jnp.sum(jnp.where(eye, own, 0.0), axis=0, keepdims=True)
    exps = [jnp.exp(own), jnp.exp(window_scores(1, 0))]
    pass_on(2, 0)
    pass_on(2, 1)
    upper = jnp.exp(window_scores(2, 0, (0, half), 2))
    pass_on(2, 2)
    pass_on(2, 3)
    lower = jnp.exp(window_scores(2, 0, (half, half), 2))
    far = jnp.sum(upper[:, rows:], axis=0, keepdims=True) + jnp.sum(lower[:, rows:], axis=0, keepdims=True)
    side_send[...] = jnp.broadcast_to(far, side_send.shape)
    side = remote(side_send, side_recv, side_sem, side_got, right)
    side.start()
    exps.append(jnp.concatenate([upper[:, :rows], lower[:, :rows]], axis=0))
    near = sum(jnp.sum(e, axis=0, keepdims=True) for e in exps)

    all_others(t_recv, t_sem, t_got).wait_recv()
    t = lax.fori_loop(0, n, lambda i, total: total + t_recv[i], jnp.zeros((8, rows), jnp.float32)) / TEMP
    exp_t = jnp.exp(t)
    side.wait_recv()
    partition = near + side_recv[:1] + sum(exp_t[k : k + 1] for k in range(neg))
    inverse = 1.0 / partition
    v = (exp_t[:neg] * inverse).astype(jnp.bfloat16).astype(jnp.float32)
    own_v = jnp.sum(jnp.where(own_entry, v, 0.0), axis=0, keepdims=True)
    v = jnp.where(own_entry, -v, v)
    merged = [v[k : k + 1] for k in range(neg)]
    for k in range(neg):
        for j in range(k + 1, neg):
            merged[k] = merged[k] + jnp.where(flat[j : j + 1] == flat[k : k + 1], v[j : j + 1], 0.0)
    v = jnp.concatenate(merged, axis=0)
    shared[0] = jnp.concatenate([v, jnp.broadcast_to(inverse, (8 - neg, rows))], axis=0)

    def sh_copy(i):
        return remote(shared.at[0], shared.at[i], sh_sem, sh_sems.at[i], ahead(i))

    def start_sh(i, carry):
        sh_copy(i).start()
        return carry

    lax.fori_loop(1, n, start_sh, 0)
    loss_ref[...] = jnp.log(partition) - positive
    for stop in range(STOPS - 1):
        weight = exps[stop] * inverse
        if stop == 0:
            weight = (weight - jnp.where(eye, 1.0, 0.0)).astype(jnp.bfloat16).astype(jnp.float32)
            p_weight[0] = weight.astype(jnp.bfloat16)
            weight = weight + jnp.where(eye, own_v, 0.0)
        q_weight[stop] = weight.T.astype(jnp.bfloat16)

    def spread(step, carry):
        grads = []
        for part in range(2):
            pos = 2 * step + part

            @pl.when(pos > 0)
            def _():
                sh_copy(pos).wait_recv()

            place = lax.broadcasted_iota(jnp.int32, (places, rows), 0)
            slot = places_of(pos)
            weight = jnp.zeros((places, rows), jnp.float32)
            for k in reversed(range(neg)):
                weight = jnp.where(place == slot[k : k + 1], shared[pos, k : k + 1, :], weight)
            q_side = jnp.maximum(weight, 0.0).astype(jnp.bfloat16)
            p_side = jnp.abs(weight).astype(jnp.bfloat16)
            q_part[pos] = dot(q_side, table[pos], TN)
            grads.append((dot(p_side, w[pos]) / TEMP).reshape(n, SLOTS, 128))
        both = jnp.concatenate(grads, axis=1).astype(jnp.bfloat16)
        sums[:, pl.ds(pl.multiple_of(step * 16, 16), 16), :] = both
        return carry

    lax.fori_loop(0, n // 2, spread, 0)

    def y_copy(pos):
        return remote(y_send.at[pos], y_recv.at[n - pos], y_sem, y_got, behind(pos))

    def gather_tile(pos):
        asked = asks_t[pl.ds(behind(pos), 1), :]
        target = lax.broadcasted_iota(jnp.int32, (rows, places), 0).astype(jnp.float32)
        hot = jnp.where(target == asked, 1.0, 0.0).astype(jnp.bfloat16)
        p_grad = dot(hot, sums[pos])
        lane = lax.broadcasted_iota(jnp.int32, p_grad.shape, 1)
        return jnp.where(lane < 64, p_grad, q_part[pos] / TEMP).astype(jnp.bfloat16)

    def gather_step(pos, carry):
        y_send[pos] = gather_tile(pos)
        y_copy(pos).start()
        return carry

    lax.fori_loop(1, n, gather_step, 0)
    y_recv[0] = gather_tile(0)

    for part in range(PARTS):
        pass_on(3, part)

    def inverse_of(stop):
        return shared[position(lax.rem(me + stop, n)), neg : neg + 1, :]

    for stop in range(1, STOPS):
        p_weight[stop] = (jnp.exp(window_scores(0, stop)) * inverse_of(stop)).astype(jnp.bfloat16)
    q_weight[STOPS - 1] = (jnp.exp(window_scores(STOPS - 1, 0)) * inverse).T.astype(jnp.bfloat16)

    def products(tile, carry):
        cut = pl.ds(pl.multiple_of(tile * 256, 256), 256)
        q_grad = jnp.zeros((rows, 256), jnp.float32)
        p_grad = jnp.zeros((rows, 256), jnp.float32)
        for stop in range(STOPS):
            q_grad = q_grad + dot(q_weight[stop], p_win[stop, :, cut])
            p_grad = p_grad + dot(p_weight[stop], q_win[stop, :, cut])
        q_acc[:, cut] = q_grad / TEMP
        p_acc[:, cut] = p_grad / TEMP
        return carry

    lax.fori_loop(0, width // 256, products, 0)

    all_others(y_recv, y_sem, y_got).wait_recv()

    def finish(chunk, total):
        cut = pl.ds(pl.multiple_of(chunk * 16, 16), 16)
        low = lax.broadcasted_iota(jnp.int32, (16, 128), 1) < 64
        for tile in range(tiles):
            lanes = slice(tile * 128, (tile + 1) * 128)
            even = y_recv[position(2 * tile), cut, :].astype(jnp.float32)
            odd = y_recv[position(2 * tile + 1), cut, :].astype(jnp.float32)
            p_acc[cut, lanes] += jnp.where(low, even, pltpu.roll(odd, 64, 1))
            q_acc[cut, lanes] += jnp.where(low, pltpu.roll(even, 64, 1), odd)
        for src, norm, out in ((q_ref, q_norm, q_acc), (p_ref, p_norm, p_acc)):
            hidden = src[cut, :].astype(jnp.float32)
            over = norm[cut, :1]
            gain = gain_ref[...]
            unit = hidden * gain * over
            grad = out[cut, :]
            inner = jnp.sum(unit * grad, axis=-1, keepdims=True)
            scaled = (grad - unit * inner) * over
            out[cut, :] = scaled * gain
            each = hidden * scaled
            total = total + each[:8] + each[8:]
        return total

    total = lax.fori_loop(0, rows // 16, finish, jnp.zeros((8, width), jnp.float32))

    total = jnp.sum(total, axis=0, keepdims=True)
    each = max(1, tiles // LINE)
    gain_part[...] = jnp.zeros_like(gain_part)
    for tile in range(tiles):
        gain_part[tile // each, tile % each : tile % each + 1, :] = total[:, tile * 128 : (tile + 1) * 128]
    outputs = (pltpu.make_async_copy(q_acc, q_out, out_sems.at[0]), pltpu.make_async_copy(p_acc, p_out, out_sems.at[1]))

    def near_copy(off):
        to = lax.rem(z + off, LINE)
        return remote(gain_part.at[to], gain_near.at[off], g_sems.at[0], g_got.at[0], row * LINE + to)

    size = lines * reps
    spot = row * reps + rep

    def far_copy(off):
        to = lax.rem(spot + off, size)
        return remote(
            gain_far.at[0], gain_far.at[off], g_sems.at[1], g_got.at[1], to // reps * LINE + z, lax.rem(to, reps)
        )

    def all_copy(off):
        to = lax.rem(z + off, LINE)
        return remote(gain_all.at[0], gain_all.at[off], g_sems.at[2], g_got.at[2], row * LINE + to)

    def whole(buffer, turn):
        cut = pl.ds(1, buffer.shape[0] - 1)
        return remote(buffer.at[cut], buffer.at[cut], g_sems.at[turn], g_got.at[turn], right)

    for off in range(1, LINE):
        near_copy(off).start()
    for copy in outputs:
        copy.start()
    whole(gain_near, 0).wait_recv()
    piece = gain_part[z]
    for off in range(1, LINE):
        piece = piece + gain_near[off]
    gain_far[0] = piece

    def start_far(off, carry):
        far_copy(off).start()
        return carry

    lax.fori_loop(1, size, start_far, 0)
    whole(gain_far, 1).wait_recv()
    gain_all[0] = lax.fori_loop(
        0, size, lambda i, add: add + gain_far[lax.rem(spot + size - i, size)], jnp.zeros((8, 128), jnp.float32)
    )
    for off in range(1, LINE):
        all_copy(off).start()
    whole(gain_all, 2).wait_recv()
    for tile in range(tiles):
        gain_out[tile : tile + 1, :] = gain_all[lax.rem(z + LINE - tile // each, LINE), tile % each : tile % each + 1, :]

    all_others(idx_all, idx_sem, idx_got).wait_send()
    all_others(x_send, x_sem, idx_got).wait_send()
    all_others(t_send, t_sem, t_got).wait_send()
    all_others(shared, sh_sem, idx_got).wait_send()
    all_others(y_send, y_sem, y_got).wait_send()
    side.wait_send()
    for turn in range(1, STOPS):
        for part in range(PARTS):
            for copy in hop(turn, part):
                copy.wait_send()
    for turn, buffer in enumerate((gain_near, gain_far, gain_all)):
        whole(buffer, turn).wait_send()
    for copy in outputs:
        copy.wait()


def run(q_hidden, p_hidden, gain, idx):
    n, reps = lax.axis_size("batch"), lax.axis_size("rep")
    rows, width = q_hidden.shape
    half = rows // 2
    places = n * SLOTS
    vmem, hbm = pl.BlockSpec(memory_space=pltpu.VMEM), pl.BlockSpec(memory_space=pl.ANY)
    bf16, f32 = jnp.bfloat16, jnp.float32
    dma = pltpu.SemaphoreType.DMA
    return pl.pallas_call(
        functools.partial(kernel, n, reps),
        in_specs=[hbm, hbm, vmem, vmem],
        out_specs=[hbm, hbm, vmem, vmem],
        out_shape=[
            jax.ShapeDtypeStruct((rows, width), f32),
            jax.ShapeDtypeStruct((rows, width), f32),
            jax.ShapeDtypeStruct((1, rows), f32),
            jax.ShapeDtypeStruct((width // 128, 128), f32),
        ],
        scratch_shapes=[
            pltpu.VMEM((rows, width), bf16),
            pltpu.VMEM((rows, width), bf16),
            pltpu.VMEM((rows, width), f32),
            pltpu.VMEM((rows, width), f32),
            pltpu.VMEM((STOPS, rows, width), bf16),
            pltpu.VMEM((STOPS, rows, width), bf16),
            pltpu.VMEM((n, rows, 128), bf16),
            pltpu.VMEM((n, rows, 128), bf16),
            pltpu.VMEM((n, rows, 128), bf16),
            pltpu.VMEM((n, rows, 128), bf16),
            pltpu.VMEM((n, places, 128), bf16),
            pltpu.VMEM((n, places, 128), bf16),
            pltpu.VMEM((n, rows, 128), f32),
            pltpu.VMEM((n, 2 * SLOTS, 128), bf16),
            pltpu.VMEM((places, 128), bf16),
            pltpu.VMEM((128, places), f32),
            pltpu.VMEM((n, 8, rows), f32),
            pltpu.VMEM((n, 8, rows), f32),
            pltpu.VMEM((n, 8, rows), f32),
            pltpu.VMEM((8, rows), f32),
            pltpu.VMEM((8, rows), f32),
            pltpu.VMEM((rows, 128), f32),
            pltpu.VMEM((rows, 128), f32),
            pltpu.VMEM((STOPS, rows, rows), bf16),
            pltpu.VMEM((STOPS, rows, rows), bf16),
            pltpu.VMEM((LINE, 8, 128), f32),
            pltpu.VMEM((LINE, 8, 128), f32),
            pltpu.VMEM((n // LINE * reps, 8, 128), f32),
            pltpu.VMEM((LINE, 8, 128), f32),
            dma((2,)),
            dma((2,)),
            dma,
            dma((n,)),
            dma,
            dma,
            dma,
            dma,
            dma,
            dma((n,)),
            dma,
            dma,
            dma((2, STOPS - 1, PARTS)),
            dma((2, STOPS - 1, PARTS)),
            dma,
            dma,
            dma((3,)),
            dma((3,)),
        ],
        compiler_params=pltpu.CompilerParams(
            collective_id=0, has_side_effects=True, vmem_limit_bytes=60 * MIB
        ),
        name="contrastive",
    )(q_hidden, p_hidden, gain.reshape(1, width), idx)


def local(query_hidden, passage_hidden, norm_gain, negatives):
    query_grad, passage_grad, loss, gain_grad = run(query_hidden[0], passage_hidden[0], norm_gain, negatives[0].T)
    return (query_grad[None], passage_grad[None], loss, gain_grad.reshape(norm_gain.shape))


def solution(mesh):
    return jax.shard_map(
        local,
        mesh=mesh,
        in_specs=(P("rep", "batch", None), P("rep", "batch", None), P(), P("rep", "batch", None)),
        out_specs=(P("rep", "batch", None), P("rep", "batch", None), P("rep", "batch"), P()),
        check_vma=False,
    )
```

```python
import functools

import jax
import jax.numpy as jnp
from jax import lax
from jax.experimental import pallas as pl
from jax.experimental.pallas import tpu as pltpu
from jax.sharding import PartitionSpec as P

STOPS = 4
TEMP = 0.05
EPS = 1e-06
SLOTS = 8
LINE = 8
STRIDE, UNSTRIDE = 27, 19
PARTS = 4
SECOND_HOP = (6, 20, 34, 48)
MIB = 1 << 20
MESH = pl.DeviceIdType.MESH
NT = (((1,), (1,)), ((), ()))
TN = (((0,), (0,)), ((), ()))


def dot(a, b, dims=(((1,), (0,)), ((), ()))):
    return lax.dot_general(a, b, dims, preferred_element_type=jnp.float32)


def kernel(
    n, reps, q_hbm, p_hbm, gain_ref, idx_ref, q_out, p_out, loss_ref, gain_out,
    q_ref, p_ref, q_acc, p_acc, p_win, q_win, x_send, w, y_send, y_recv, table, sums, q_part,
    idx_all, asks, asks_t, t_send, t_recv, shared, side_send, side_recv, q_norm, p_norm, q_weight, p_weight,
    gain_part, gain_near, gain_far, gain_all,
    in_sems, out_sems, x_sem, x_sems, idx_sem, idx_got, t_sem, t_got, sh_sem, sh_sems, y_sem, y_got,
    chain_sem, chain_got, side_sem, side_got, g_sems, g_got,
):
    me, rep = lax.axis_index("batch"), lax.axis_index("rep")
    rows, width = q_ref.shape
    half, quarter = rows // 2, rows // PARTS
    neg = 3
    places = n * SLOTS
    tiles = width // 128

    def ahead(i):
        return lax.rem(me + STRIDE * i, n)

    def behind(i):
        return lax.rem(me + n * STRIDE - STRIDE * i, n)

    def position(device):
        return lax.rem((me + n - device) * UNSTRIDE, n)

    def remote(src, dst, send, recv, device, group=rep):
        return pltpu.make_async_remote_copy(
            src_ref=src, dst_ref=dst, send_sem=send, recv_sem=recv, device_id=(device, group), device_id_type=MESH
        )

    inputs = (pltpu.make_async_copy(q_hbm, q_ref, in_sems.at[0]), pltpu.make_async_copy(p_hbm, p_ref, in_sems.at[1]))
    for copy in inputs:
        copy.start()

    barrier = pltpu.get_barrier_semaphore()
    z, row = lax.rem(me, LINE), me // LINE
    lines = n // LINE

    def greet(i, carry):
        pl.semaphore_signal(barrier, inc=1, device_id=(ahead(i), rep), device_id_type=MESH)
        return carry

    def greet_group(i, carry):
        group = lax.rem(rep + 1 + i // lines, reps)
        device = lax.rem(i, lines) * LINE + z
        pl.semaphore_signal(barrier, inc=1, device_id=(device, group), device_id_type=MESH)
        return carry

    lax.fori_loop(1, n, greet, 0)
    lax.fori_loop(0, (reps - 1) * lines, greet_group, 0)

    flat = idx_ref[...]
    flat_f = flat.astype(jnp.float32)
    owner_row = (flat >> 7).astype(jnp.float32)
    columns = jnp.concatenate([flat_f, jnp.zeros((rows - neg, rows), jnp.float32)], axis=0).T
    owner_columns = (columns.astype(jnp.int32) >> 7).astype(jnp.float32)
    down = lax.broadcasted_iota(jnp.int32, (rows, rows), 0)
    across = lax.broadcasted_iota(jnp.int32, (rows, rows), 1)
    again_row, again_column, ranks = [], [], []
    for k in range(neg):
        seen = jnp.zeros((rows, rows), jnp.float32)
        seen_t = jnp.zeros((rows, rows), jnp.float32)
        for j in range(k + 1):
            same = columns[:, j : j + 1] == flat_f[k : k + 1]
            same_t = columns[:, k : k + 1] == flat_f[j : j + 1]
            if j == k:
                same, same_t = same & (down < across), same_t & (across < down)
            seen = seen + jnp.where(same, 1.0, 0.0)
            seen_t = seen_t + jnp.where(same_t, 1.0, 0.0)
        again_row.append(jnp.sum(seen, axis=0, keepdims=True))
        again_column.append(jnp.sum(seen_t, axis=1, keepdims=True))
    for k in range(neg):
        count = jnp.zeros((rows, rows), jnp.float32)
        for j in range(neg):
            lower = (owner_columns[:, j : j + 1] == owner_row[k : k + 1]) & (columns[:, j : j + 1] < flat_f[k : k + 1])
            count = count + jnp.where(lower & (again_column[j] == 0.0), 1.0, 0.0)
        ranks.append(jnp.sum(count, axis=0, keepdims=True))
    named = jnp.zeros((SLOTS, 128), jnp.float32)
    at_rank = lax.broadcasted_iota(jnp.int32, (SLOTS, rows), 0).astype(jnp.float32)
    for k in range(neg):
        first = (at_rank == ranks[k]) & (again_row[k] == 0.0)
        value = jnp.where(first, (flat[k : k + 1] & 127).astype(jnp.float32) + 1.0, 0.0).astype(jnp.bfloat16)
        at_owner = jnp.where(owner_columns[:, k : k + 1] == across.astype(jnp.float32), 1.0, 0.0).astype(jnp.bfloat16)
        named = named + dot(value, at_owner)
    lines_of = [named - 1.0, owner_row] + ranks + [jnp.zeros((2, 128), jnp.float32)]
    idx_all[0] = jnp.concatenate(lines_of, axis=0).astype(jnp.bfloat16)
    own_entry = flat == me * rows + lax.broadcasted_iota(jnp.int32, flat.shape, 1)

    for copy in inputs:
        copy.wait()

    def normalize(chunk, carry):
        cut = pl.ds(pl.multiple_of(chunk * 16, 16), 16)
        units = []
        for src, win, norm in ((q_ref, q_win, q_norm), (p_ref, p_win, p_norm)):
            scaled = src[cut, :].astype(jnp.float32) * gain_ref[...]
            length = jnp.sqrt(jnp.sum(scaled * scaled, axis=-1, keepdims=True) + EPS)
            unit = scaled * (1.0 / length)
            win[0, cut, :] = unit.astype(jnp.bfloat16)
            norm[cut, :] = jnp.broadcast_to(1.0 / length, (16, 128))
            units.append(unit)
        low = lax.broadcasted_iota(jnp.int32, (16, 128), 1) < 64
        for tile in range(tiles):
            q_tile = units[0][:, tile * 128 : (tile + 1) * 128]
            p_tile = units[1][:, tile * 128 : (tile + 1) * 128]
            x_send[2 * tile, cut, :] = jnp.where(low, q_tile, pltpu.roll(p_tile, 64, 1)).astype(jnp.bfloat16)
            x_send[2 * tile + 1, cut, :] = jnp.where(low, pltpu.roll(q_tile, 64, 1), p_tile).astype(jnp.bfloat16)
        return carry

    lax.fori_loop(0, rows // 16, normalize, 0)
    w[0] = x_send[me]
    pl.semaphore_wait(barrier, n - 1 + (reps - 1) * lines)

    def start_idx(i, carry):
        remote(idx_all.at[0], idx_all.at[i], idx_sem, idx_got, ahead(i)).start()
        return carry

    lax.fori_loop(1, n, start_idx, 0)

    def x_copy(i):
        return remote(x_send.at[ahead(i)], w.at[i], x_sem, x_sems.at[i], ahead(i))

    def start_x(i, carry):
        x_copy(i).start()
        return carry

    lax.fori_loop(1, n, start_x, 0)

    right, left = lax.rem(me + 1, n), lax.rem(me + n - 1, n)

    def hop(turn, part):
        cut = pl.ds(part * quarter, quarter)
        sems = [(chain_sem.at[way, turn - 1, part], chain_got.at[way, turn - 1, part]) for way in range(2)]
        return (
            remote(p_win.at[turn - 1, cut], p_win.at[turn, cut], *sems[0], right),
            remote(q_win.at[turn - 1, cut], q_win.at[turn, cut], *sems[1], left),
        )

    def start_hop(turn, part):
        for copy in hop(turn, part):
            copy.start()

    def end_hop(turn, part):
        for copy in hop(turn, part):
            copy.wait_recv()

    for part in range(PARTS):
        start_hop(1, part)

    others = pl.ds(1, n - 1)

    def all_others(buffer, send, recv):
        return remote(buffer.at[others], buffer.at[others], send, recv, right)

    all_others(idx_all, idx_sem, idx_got).wait_recv()
    wide = idx_all[...].astype(jnp.float32)[:, :SLOTS, :].reshape(places, 128)
    asks[...] = wide.astype(jnp.bfloat16)
    asks_t[...] = wide.T

    def pick(step, carry):
        picked = []
        for part in range(2):
            pos = 2 * step + part

            @pl.when(pos > 0)
            def _():
                x_copy(pos).wait_recv()

            owner = behind(pos)
            column = (lax.broadcasted_iota(jnp.int32, (128, 128), 0) == owner).astype(jnp.bfloat16)
            asked = dot(asks[...], column)
            lane = lax.broadcasted_iota(jnp.int32, asked.shape, 1).astype(jnp.float32)
            hot = jnp.where(asked == lane, 1.0, 0.0).astype(jnp.bfloat16)
            picked.append(dot(hot, w[pos]).reshape(n, SLOTS, 128))
        both = jnp.concatenate(picked, axis=1).astype(jnp.bfloat16)
        table[:, pl.ds(pl.multiple_of(step * 16, 16), 16), :] = both
        return carry

    lax.fori_loop(0, n // 2, pick, 0)

    def places_of(pos):
        entry = idx_all[pos].astype(jnp.float32).astype(jnp.int32)
        owner, rank = entry[SLOTS : SLOTS + neg], entry[SLOTS + neg : SLOTS + 2 * neg]
        return (((me + n - owner) * UNSTRIDE) & (n - 1)) * SLOTS + rank

    def t_copy(pos):
        return remote(t_send.at[pos], t_recv.at[n - pos], t_sem, t_got, behind(pos))

    def partial_scores(pos):
        mine = w[pos].astype(jnp.float32)
        lane = lax.broadcasted_iota(jnp.int32, mine.shape, 1)
        query = jnp.where(lane < 64, 0.0, pltpu.roll(mine, 64, 1)).astype(jnp.bfloat16)
        scores = dot(table[pos], query, NT)
        place = lax.broadcasted_iota(jnp.int32, scores.shape, 0)
        slot = places_of(pos)
        parts = [
            jnp.sum(jnp.where(place == slot[k : k + 1], scores, 0.0), axis=0, keepdims=True) for k in range(neg)
        ]
        return jnp.concatenate(parts + [jnp.zeros((8 - neg, rows), jnp.float32)], axis=0)

    def score_step(pos, carry):
        for part in range(PARTS):

            @pl.when(pos == max(1, SECOND_HOP[part] * n // 64))
            def _():
                end_hop(1, part)
                start_hop(2, part)

        t_send[pos] = partial_scores(pos)
        t_copy(pos).start()
        return carry

    lax.fori_loop(1, n, score_step, 0)
    t_recv[0] = partial_scores(0)

    def window_scores(p_slot, q_slot, p_rows=(0, rows), q_count=1):
        step = 512

        def add(tile, total):
            cut = pl.ds(pl.multiple_of(tile * step, step), step)
            down_block = p_win[p_slot, p_rows[0] : p_rows[0] + p_rows[1], cut]
            across_block = q_win[q_slot : q_slot + q_count, :, cut].reshape(q_count * rows, step)
            return total + dot(down_block, across_block, NT)

        start = jnp.zeros((p_rows[1], q_count * rows), jnp.float32)
        return lax.fori_loop(0, width // step, add, start) / TEMP

    own = window_scores(0, 0)
    eye = down == across
    positive = jnp.sum(jnp.where(eye, own, 0.0), axis=0, keepdims=True)
    exps = [jnp.exp(own), jnp.exp(window_scores(1, 0))]
    end_hop(2, 0)
    end_hop(2, 1)
    upper = jnp.exp(window_scores(2, 0, (0, half), 2))
    end_hop(2, 2)
    end_hop(2, 3)
    lower = jnp.exp(window_scores(2, 0, (half, half), 2))
    far = jnp.sum(upper[:, rows:], axis=0, keepdims=True) + jnp.sum(lower[:, rows:], axis=0, keepdims=True)
    side_send[...] = jnp.broadcast_to(far, side_send.shape)
    side = remote(side_send, side_recv, side_sem, side_got, right)
    side.start()
    exps.append(jnp.concatenate([upper[:, :rows], lower[:, :rows]], axis=0))
    near = sum(jnp.sum(e, axis=0, keepdims=True) for e in exps)

    all_others(t_recv, t_sem, t_got).wait_recv()
    t = lax.fori_loop(0, n, lambda i, total: total + t_recv[i], jnp.zeros((8, rows), jnp.float32)) / TEMP
    exp_t = jnp.exp(t)
    side.wait_recv()
    partition = near + side_recv[:1] + sum(exp_t[k : k + 1] for k in range(neg))
    inverse = 1.0 / partition
    v = (exp_t[:neg] * inverse).astype(jnp.bfloat16).astype(jnp.float32)
    own_v = jnp.sum(jnp.where(own_entry, v, 0.0), axis=0, keepdims=True)
    v = jnp.where(own_entry, -v, v)
    merged = [v[k : k + 1] for k in range(neg)]
    for k in range(neg):
        for j in range(k + 1, neg):
            merged[k] = merged[k] + jnp.where(flat[j : j + 1] == flat[k : k + 1], v[j : j + 1], 0.0)
    v = jnp.concatenate(merged, axis=0)
    shared[0] = jnp.concatenate([v, jnp.broadcast_to(inverse, (8 - neg, rows))], axis=0)

    def sh_copy(i):
        return remote(shared.at[0], shared.at[i], sh_sem, sh_sems.at[i], ahead(i))

    def start_sh(i, carry):
        sh_copy(i).start()
        return carry

    lax.fori_loop(1, n, start_sh, 0)
    for part in range(PARTS):
        start_hop(3, part)
    loss_ref[...] = jnp.log(partition) - positive
    for stop in range(STOPS - 1):
        weight = exps[stop] * inverse
        if stop == 0:
            weight = (weight - jnp.where(eye, 1.0, 0.0)).astype(jnp.bfloat16).astype(jnp.float32)
            p_weight[0] = weight.astype(jnp.bfloat16)
            weight = weight + jnp.where(eye, own_v, 0.0)
        q_weight[stop] = weight.T.astype(jnp.bfloat16)

    def spread(step, carry):
        grads = []
        for part in range(2):
            pos = 2 * step + part

            @pl.when(pos > 0)
            def _():
                sh_copy(pos).wait_recv()

            place = lax.broadcasted_iota(jnp.int32, (places, rows), 0)
            slot = places_of(pos)
            weight = jnp.zeros((places, rows), jnp.float32)
            for k in reversed(range(neg)):
                weight = jnp.where(place == slot[k : k + 1], shared[pos, k : k + 1, :], weight)
            q_side = jnp.maximum(weight, 0.0).astype(jnp.bfloat16)
            p_side = jnp.abs(weight).astype(jnp.bfloat16)
            q_part[pos] = dot(q_side, table[pos], TN)
            grads.append((dot(p_side, w[pos]) / TEMP).reshape(n, SLOTS, 128))
        both = jnp.concatenate(grads, axis=1).astype(jnp.bfloat16)
        sums[:, pl.ds(pl.multiple_of(step * 16, 16), 16), :] = both
        return carry

    lax.fori_loop(0, n // 2, spread, 0)

    def y_copy(pos):
        return remote(y_send.at[pos], y_recv.at[n - pos], y_sem, y_got, behind(pos))

    def gather_tile(pos):
        asked = asks_t[pl.ds(behind(pos), 1), :]
        target = lax.broadcasted_iota(jnp.int32, (rows, places), 0).astype(jnp.float32)
        hot = jnp.where(target == asked, 1.0, 0.0).astype(jnp.bfloat16)
        p_grad = dot(hot, sums[pos])
        lane = lax.broadcasted_iota(jnp.int32, p_grad.shape, 1)
        return jnp.where(lane < 64, p_grad, q_part[pos] / TEMP).astype(jnp.bfloat16)

    def gather_step(pos, carry):
        y_send[pos] = gather_tile(pos)
        y_copy(pos).start()
        return carry

    lax.fori_loop(1, n, gather_step, 0)
    y_recv[0] = gather_tile(0)

    for part in range(PARTS):
        end_hop(3, part)

    def inverse_of(stop):
        return shared[position(lax.rem(me + stop, n)), neg : neg + 1, :]

    for stop in range(1, STOPS):
        p_weight[stop] = (jnp.exp(window_scores(0, stop)) * inverse_of(stop)).astype(jnp.bfloat16)
    q_weight[STOPS - 1] = (jnp.exp(window_scores(STOPS - 1, 0)) * inverse).T.astype(jnp.bfloat16)

    def products(tile, carry):
        cut = pl.ds(pl.multiple_of(tile * 256, 256), 256)
        q_grad = jnp.zeros((rows, 256), jnp.float32)
        p_grad = jnp.zeros((rows, 256), jnp.float32)
        for stop in range(STOPS):
            q_grad = q_grad + dot(q_weight[stop], p_win[stop, :, cut])
            p_grad = p_grad + dot(p_weight[stop], q_win[stop, :, cut])
        q_acc[:, cut] = q_grad / TEMP
        p_acc[:, cut] = p_grad / TEMP
        return carry

    lax.fori_loop(0, width // 256, products, 0)

    all_others(y_recv, y_sem, y_got).wait_recv()

    def finish(chunk, total):
        cut = pl.ds(pl.multiple_of(chunk * 16, 16), 16)
        low = lax.broadcasted_iota(jnp.int32, (16, 128), 1) < 64
        for tile in range(tiles):
            lanes = slice(tile * 128, (tile + 1) * 128)
            even = y_recv[position(2 * tile), cut, :].astype(jnp.float32)
            odd = y_recv[position(2 * tile + 1), cut, :].astype(jnp.float32)
            p_acc[cut, lanes] += jnp.where(low, even, pltpu.roll(odd, 64, 1))
            q_acc[cut, lanes] += jnp.where(low, pltpu.roll(even, 64, 1), odd)
        for src, norm, out in ((q_ref, q_norm, q_acc), (p_ref, p_norm, p_acc)):
            hidden = src[cut, :].astype(jnp.float32)
            over = norm[cut, :1]
            gain = gain_ref[...]
            unit = hidden * gain * over
            grad = out[cut, :]
            inner = jnp.sum(unit * grad, axis=-1, keepdims=True)
            scaled = (grad - unit * inner) * over
            out[cut, :] = scaled * gain
            each = hidden * scaled
            total = total + each[:8] + each[8:]
        return total

    total = lax.fori_loop(0, rows // 16, finish, jnp.zeros((8, width), jnp.float32))

    total = jnp.sum(total, axis=0, keepdims=True)
    each = max(1, tiles // LINE)
    gain_part[...] = jnp.zeros_like(gain_part)
    for tile in range(tiles):
        gain_part[tile // each, tile % each : tile % each + 1, :] = total[:, tile * 128 : (tile + 1) * 128]
    outputs = (pltpu.make_async_copy(q_acc, q_out, out_sems.at[0]), pltpu.make_async_copy(p_acc, p_out, out_sems.at[1]))

    def near_copy(off):
        to = lax.rem(z + off, LINE)
        return remote(gain_part.at[to], gain_near.at[off], g_sems.at[0], g_got.at[0], row * LINE + to)

    size = lines * reps
    spot = row * reps + rep

    def far_copy(off):
        to = lax.rem(spot + off, size)
        return remote(
            gain_far.at[0], gain_far.at[off], g_sems.at[1], g_got.at[1], to // reps * LINE + z, lax.rem(to, reps)
        )

    def all_copy(off):
        to = lax.rem(z + off, LINE)
        return remote(gain_all.at[0], gain_all.at[off], g_sems.at[2], g_got.at[2], row * LINE + to)

    def whole(buffer, turn):
        cut = pl.ds(1, buffer.shape[0] - 1)
        return remote(buffer.at[cut], buffer.at[cut], g_sems.at[turn], g_got.at[turn], right)

    for off in range(1, LINE):
        near_copy(off).start()
    for copy in outputs:
        copy.start()
    whole(gain_near, 0).wait_recv()
    piece = gain_part[z]
    for off in range(1, LINE):
        piece = piece + gain_near[off]
    gain_far[0] = piece

    def start_far(off, carry):
        far_copy(off).start()
        return carry

    lax.fori_loop(1, size, start_far, 0)
    whole(gain_far, 1).wait_recv()
    gain_all[0] = lax.fori_loop(
        0, size, lambda i, add: add + gain_far[lax.rem(spot + size - i, size)], jnp.zeros((8, 128), jnp.float32)
    )
    for off in range(1, LINE):
        all_copy(off).start()
    whole(gain_all, 2).wait_recv()
    for tile in range(tiles):
        gain_out[tile : tile + 1, :] = gain_all[lax.rem(z + LINE - tile // each, LINE), tile % each : tile % each + 1, :]

    all_others(idx_all, idx_sem, idx_got).wait_send()
    all_others(x_send, x_sem, idx_got).wait_send()
    all_others(t_send, t_sem, t_got).wait_send()
    all_others(shared, sh_sem, idx_got).wait_send()
    all_others(y_send, y_sem, y_got).wait_send()
    side.wait_send()
    for turn in range(1, STOPS):
        for part in range(PARTS):
            for copy in hop(turn, part):
                copy.wait_send()
    for turn, buffer in enumerate((gain_near, gain_far, gain_all)):
        whole(buffer, turn).wait_send()
    for copy in outputs:
        copy.wait()


def run(q_hidden, p_hidden, gain, idx):
    n, reps = lax.axis_size("batch"), lax.axis_size("rep")
    rows, width = q_hidden.shape
    half = rows // 2
    places = n * SLOTS
    vmem, hbm = pl.BlockSpec(memory_space=pltpu.VMEM), pl.BlockSpec(memory_space=pl.ANY)
    bf16, f32 = jnp.bfloat16, jnp.float32
    dma = pltpu.SemaphoreType.DMA
    return pl.pallas_call(
        functools.partial(kernel, n, reps),
        in_specs=[hbm, hbm, vmem, vmem],
        out_specs=[hbm, hbm, vmem, vmem],
        out_shape=[
            jax.ShapeDtypeStruct((rows, width), f32),
            jax.ShapeDtypeStruct((rows, width), f32),
            jax.ShapeDtypeStruct((1, rows), f32),
            jax.ShapeDtypeStruct((width // 128, 128), f32),
        ],
        scratch_shapes=[
            pltpu.VMEM((rows, width), bf16),
            pltpu.VMEM((rows, width), bf16),
            pltpu.VMEM((rows, width), f32),
            pltpu.VMEM((rows, width), f32),
            pltpu.VMEM((STOPS, rows, width), bf16),
            pltpu.VMEM((STOPS, rows, width), bf16),
            pltpu.VMEM((n, rows, 128), bf16),
            pltpu.VMEM((n, rows, 128), bf16),
            pltpu.VMEM((n, rows, 128), bf16),
            pltpu.VMEM((n, rows, 128), bf16),
            pltpu.VMEM((n, places, 128), bf16),
            pltpu.VMEM((n, places, 128), bf16),
            pltpu.VMEM((n, rows, 128), f32),
            pltpu.VMEM((n, 2 * SLOTS, 128), bf16),
            pltpu.VMEM((places, 128), bf16),
            pltpu.VMEM((128, places), f32),
            pltpu.VMEM((n, 8, rows), f32),
            pltpu.VMEM((n, 8, rows), f32),
            pltpu.VMEM((n, 8, rows), f32),
            pltpu.VMEM((8, rows), f32),
            pltpu.VMEM((8, rows), f32),
            pltpu.VMEM((rows, 128), f32),
            pltpu.VMEM((rows, 128), f32),
            pltpu.VMEM((STOPS, rows, rows), bf16),
            pltpu.VMEM((STOPS, rows, rows), bf16),
            pltpu.VMEM((LINE, 8, 128), f32),
            pltpu.VMEM((LINE, 8, 128), f32),
            pltpu.VMEM((n // LINE * reps, 8, 128), f32),
            pltpu.VMEM((LINE, 8, 128), f32),
            dma((2,)),
            dma((2,)),
            dma,
            dma((n,)),
            dma,
            dma,
            dma,
            dma,
            dma,
            dma((n,)),
            dma,
            dma,
            dma((2, STOPS - 1, PARTS)),
            dma((2, STOPS - 1, PARTS)),
            dma,
            dma,
            dma((3,)),
            dma((3,)),
        ],
        compiler_params=pltpu.CompilerParams(
            collective_id=0, has_side_effects=True, vmem_limit_bytes=60 * MIB
        ),
        name="contrastive",
    )(q_hidden, p_hidden, gain.reshape(1, width), idx)


def local(query_hidden, passage_hidden, norm_gain, negatives):
    query_grad, passage_grad, loss, gain_grad = run(query_hidden[0], passage_hidden[0], norm_gain, negatives[0].T)
    return (query_grad[None], passage_grad[None], loss, gain_grad.reshape(norm_gain.shape))


def solution(mesh):
    return jax.shard_map(
        local,
        mesh=mesh,
        in_specs=(P("rep", "batch", None), P("rep", "batch", None), P(), P("rep", "batch", None)),
        out_specs=(P("rep", "batch", None), P("rep", "batch", None), P("rep", "batch"), P()),
        check_vma=False,
    )
```

```python
import functools

import jax
import jax.numpy as jnp
from jax import lax
from jax.experimental import pallas as pl
from jax.experimental.pallas import tpu as pltpu
from jax.sharding import PartitionSpec as P

STOPS = 4
TEMP = 0.05
EPS = 1e-06
SLOTS = 8
LINE = 8
STRIDE, UNSTRIDE = 27, 19
PARTS = 4
SECOND_HOP = (1, 2, 3, 4)
MIB = 1 << 20
MESH = pl.DeviceIdType.MESH
NT = (((1,), (1,)), ((), ()))
TN = (((0,), (0,)), ((), ()))


def dot(a, b, dims=(((1,), (0,)), ((), ()))):
    return lax.dot_general(a, b, dims, preferred_element_type=jnp.float32)


def kernel(
    n, reps, q_hbm, p_hbm, gain_ref, idx_ref, q_out, p_out, loss_ref, gain_out,
    q_ref, p_ref, q_acc, p_acc, p_win, q_win, x_send, w, y_send, y_recv, table, sums, q_part,
    idx_all, asks, asks_t, t_send, t_recv, shared, side_send, side_recv, q_norm, p_norm, q_weight, p_weight,
    gain_part, gain_near, gain_far, gain_all,
    in_sems, out_sems, x_sem, x_sems, idx_sem, idx_got, t_sem, t_got, sh_sem, sh_sems, y_sem, y_got,
    chain_sem, chain_got, side_sem, side_got, g_sems, g_got,
):
    me, rep = lax.axis_index("batch"), lax.axis_index("rep")
    rows, width = q_ref.shape
    half, quarter = rows // 2, rows // PARTS
    neg = 3
    places = n * SLOTS
    tiles = width // 128

    def ahead(i):
        return lax.rem(me + STRIDE * i, n)

    def behind(i):
        return lax.rem(me + n * STRIDE - STRIDE * i, n)

    def position(device):
        return lax.rem((me + n - device) * UNSTRIDE, n)

    def remote(src, dst, send, recv, device, group=rep):
        return pltpu.make_async_remote_copy(
            src_ref=src, dst_ref=dst, send_sem=send, recv_sem=recv, device_id=(device, group), device_id_type=MESH
        )

    inputs = (pltpu.make_async_copy(q_hbm, q_ref, in_sems.at[0]), pltpu.make_async_copy(p_hbm, p_ref, in_sems.at[1]))
    for copy in inputs:
        copy.start()

    barrier = pltpu.get_barrier_semaphore()
    z, row = lax.rem(me, LINE), me // LINE
    lines = n // LINE

    def greet(i, carry):
        pl.semaphore_signal(barrier, inc=1, device_id=(ahead(i), rep), device_id_type=MESH)
        return carry

    def greet_group(i, carry):
        group = lax.rem(rep + 1 + i // lines, reps)
        device = lax.rem(i, lines) * LINE + z
        pl.semaphore_signal(barrier, inc=1, device_id=(device, group), device_id_type=MESH)
        return carry

    lax.fori_loop(1, n, greet, 0)
    lax.fori_loop(0, (reps - 1) * lines, greet_group, 0)

    flat = idx_ref[...]
    flat_f = flat.astype(jnp.float32)
    owner_row = (flat >> 7).astype(jnp.float32)
    columns = jnp.concatenate([flat_f, jnp.zeros((rows - neg, rows), jnp.float32)], axis=0).T
    owner_columns = (columns.astype(jnp.int32) >> 7).astype(jnp.float32)
    down = lax.broadcasted_iota(jnp.int32, (rows, rows), 0)
    across = lax.broadcasted_iota(jnp.int32, (rows, rows), 1)
    again_row, again_column, ranks = [], [], []
    for k in range(neg):
        seen = jnp.zeros((rows, rows), jnp.float32)
        seen_t = jnp.zeros((rows, rows), jnp.float32)
        for j in range(k + 1):
            same = columns[:, j : j + 1] == flat_f[k : k + 1]
            same_t = columns[:, k : k + 1] == flat_f[j : j + 1]
            if j == k:
                same, same_t = same & (down < across), same_t & (across < down)
            seen = seen + jnp.where(same, 1.0, 0.0)
            seen_t = seen_t + jnp.where(same_t, 1.0, 0.0)
        again_row.append(jnp.sum(seen, axis=0, keepdims=True))
        again_column.append(jnp.sum(seen_t, axis=1, keepdims=True))
    for k in range(neg):
        count = jnp.zeros((rows, rows), jnp.float32)
        for j in range(neg):
            lower = (owner_columns[:, j : j + 1] == owner_row[k : k + 1]) & (columns[:, j : j + 1] < flat_f[k : k + 1])
            count = count + jnp.where(lower & (again_column[j] == 0.0), 1.0, 0.0)
        ranks.append(jnp.sum(count, axis=0, keepdims=True))
    named = jnp.zeros((SLOTS, 128), jnp.float32)
    at_rank = lax.broadcasted_iota(jnp.int32, (SLOTS, rows), 0).astype(jnp.float32)
    for k in range(neg):
        first = (at_rank == ranks[k]) & (again_row[k] == 0.0)
        value = jnp.where(first, (flat[k : k + 1] & 127).astype(jnp.float32) + 1.0, 0.0).astype(jnp.bfloat16)
        at_owner = jnp.where(owner_columns[:, k : k + 1] == across.astype(jnp.float32), 1.0, 0.0).astype(jnp.bfloat16)
        named = named + dot(value, at_owner)
    lines_of = [named - 1.0, owner_row] + ranks + [jnp.zeros((2, 128), jnp.float32)]
    idx_all[0] = jnp.concatenate(lines_of, axis=0).astype(jnp.bfloat16)
    own_entry = flat == me * rows + lax.broadcasted_iota(jnp.int32, flat.shape, 1)

    for copy in inputs:
        copy.wait()

    def normalize(chunk, carry):
        cut = pl.ds(pl.multiple_of(chunk * 16, 16), 16)
        units = []
        for src, win, norm in ((q_ref, q_win, q_norm), (p_ref, p_win, p_norm)):
            scaled = src[cut, :].astype(jnp.float32) * gain_ref[...]
            length = jnp.sqrt(jnp.sum(scaled * scaled, axis=-1, keepdims=True) + EPS)
            unit = scaled * (1.0 / length)
            win[0, cut, :] = unit.astype(jnp.bfloat16)
            norm[cut, :] = jnp.broadcast_to(1.0 / length, (16, 128))
            units.append(unit)
        low = lax.broadcasted_iota(jnp.int32, (16, 128), 1) < 64
        for tile in range(tiles):
            q_tile = units[0][:, tile * 128 : (tile + 1) * 128]
            p_tile = units[1][:, tile * 128 : (tile + 1) * 128]
            x_send[2 * tile, cut, :] = jnp.where(low, q_tile, pltpu.roll(p_tile, 64, 1)).astype(jnp.bfloat16)
            x_send[2 * tile + 1, cut, :] = jnp.where(low, pltpu.roll(q_tile, 64, 1), p_tile).astype(jnp.bfloat16)
        return carry

    lax.fori_loop(0, rows // 16, normalize, 0)
    w[0] = x_send[me]
    pl.semaphore_wait(barrier, n - 1 + (reps - 1) * lines)

    def start_idx(i, carry):
        remote(idx_all.at[0], idx_all.at[i], idx_sem, idx_got, ahead(i)).start()
        return carry

    lax.fori_loop(1, n, start_idx, 0)

    def x_copy(i):
        return remote(x_send.at[ahead(i)], w.at[i], x_sem, x_sems.at[i], ahead(i))

    def start_x(i, carry):
        x_copy(i).start()
        return carry

    lax.fori_loop(1, n, start_x, 0)

    right, left = lax.rem(me + 1, n), lax.rem(me + n - 1, n)

    def hop(turn, part):
        cut = pl.ds(part * quarter, quarter)
        sems = [(chain_sem.at[way, turn - 1, part], chain_got.at[way, turn - 1, part]) for way in range(2)]
        return (
            remote(p_win.at[turn - 1, cut], p_win.at[turn, cut], *sems[0], right),
            remote(q_win.at[turn - 1, cut], q_win.at[turn, cut], *sems[1], left),
        )

    def start_hop(turn, part):
        for copy in hop(turn, part):
            copy.start()

    def end_hop(turn, part):
        for copy in hop(turn, part):
            copy.wait_recv()

    for part in range(PARTS):
        start_hop(1, part)

    others = pl.ds(1, n - 1)

    def all_others(buffer, send, recv):
        return remote(buffer.at[others], buffer.at[others], send, recv, right)

    all_others(idx_all, idx_sem, idx_got).wait_recv()
    wide = idx_all[...].astype(jnp.float32)[:, :SLOTS, :].reshape(places, 128)
    asks[...] = wide.astype(jnp.bfloat16)
    asks_t[...] = wide.T

    def pick(step, carry):
        picked = []
        for part in range(2):
            pos = 2 * step + part

            @pl.when(pos > 0)
            def _():
                x_copy(pos).wait_recv()

            owner = behind(pos)
            column = (lax.broadcasted_iota(jnp.int32, (128, 128), 0) == owner).astype(jnp.bfloat16)
            asked = dot(asks[...], column)
            lane = lax.broadcasted_iota(jnp.int32, asked.shape, 1).astype(jnp.float32)
            hot = jnp.where(asked == lane, 1.0, 0.0).astype(jnp.bfloat16)
            picked.append(dot(hot, w[pos]).reshape(n, SLOTS, 128))
        both = jnp.concatenate(picked, axis=1).astype(jnp.bfloat16)
        table[:, pl.ds(pl.multiple_of(step * 16, 16), 16), :] = both
        return carry

    lax.fori_loop(0, n // 2, pick, 0)

    def places_of(pos):
        entry = idx_all[pos].astype(jnp.float32).astype(jnp.int32)
        owner, rank = entry[SLOTS : SLOTS + neg], entry[SLOTS + neg : SLOTS + 2 * neg]
        return (((me + n - owner) * UNSTRIDE) & (n - 1)) * SLOTS + rank

    def t_copy(pos):
        return remote(t_send.at[pos], t_recv.at[n - pos], t_sem, t_got, behind(pos))

    def partial_scores(pos):
        mine = w[pos].astype(jnp.float32)
        lane = lax.broadcasted_iota(jnp.int32, mine.shape, 1)
        query = jnp.where(lane < 64, 0.0, pltpu.roll(mine, 64, 1)).astype(jnp.bfloat16)
        scores = dot(table[pos], query, NT)
        place = lax.broadcasted_iota(jnp.int32, scores.shape, 0)
        slot = places_of(pos)
        parts = [
            jnp.sum(jnp.where(place == slot[k : k + 1], scores, 0.0), axis=0, keepdims=True) for k in range(neg)
        ]
        return jnp.concatenate(parts + [jnp.zeros((8 - neg, rows), jnp.float32)], axis=0)

    def score_step(pos, carry):
        for part in range(PARTS):

            @pl.when(pos == max(1, SECOND_HOP[part] * n // 64))
            def _():
                end_hop(1, part)
                start_hop(2, part)

        t_send[pos] = partial_scores(pos)
        t_copy(pos).start()
        return carry

    lax.fori_loop(1, n, score_step, 0)
    t_recv[0] = partial_scores(0)

    def window_scores(p_slot, q_slot, p_rows=(0, rows), q_count=1):
        step = 512

        def add(tile, total):
            cut = pl.ds(pl.multiple_of(tile * step, step), step)
            down_block = p_win[p_slot, p_rows[0] : p_rows[0] + p_rows[1], cut]
            across_block = q_win[q_slot : q_slot + q_count, :, cut].reshape(q_count * rows, step)
            return total + dot(down_block, across_block, NT)

        start = jnp.zeros((p_rows[1], q_count * rows), jnp.float32)
        return lax.fori_loop(0, width // step, add, start) / TEMP

    own = window_scores(0, 0)
    eye = down == across
    positive = jnp.sum(jnp.where(eye, own, 0.0), axis=0, keepdims=True)
    exps = [jnp.exp(own), jnp.exp(window_scores(1, 0))]
    end_hop(2, 0)
    end_hop(2, 1)
    upper = jnp.exp(window_scores(2, 0, (0, half), 2))
    end_hop(2, 2)
    end_hop(2, 3)
    lower = jnp.exp(window_scores(2, 0, (half, half), 2))
    far = jnp.sum(upper[:, rows:], axis=0, keepdims=True) + jnp.sum(lower[:, rows:], axis=0, keepdims=True)
    side_send[...] = jnp.broadcast_to(far, side_send.shape)
    side = remote(side_send, side_recv, side_sem, side_got, right)
    side.start()
    exps.append(jnp.concatenate([upper[:, :rows], lower[:, :rows]], axis=0))
    near = sum(jnp.sum(e, axis=0, keepdims=True) for e in exps)

    all_others(t_recv, t_sem, t_got).wait_recv()
    t = lax.fori_loop(0, n, lambda i, total: total + t_recv[i], jnp.zeros((8, rows), jnp.float32)) / TEMP
    exp_t = jnp.exp(t)
    side.wait_recv()
    partition = near + side_recv[:1] + sum(exp_t[k : k + 1] for k in range(neg))
    inverse = 1.0 / partition
    v = (exp_t[:neg] * inverse).astype(jnp.bfloat16).astype(jnp.float32)
    own_v = jnp.sum(jnp.where(own_entry, v, 0.0), axis=0, keepdims=True)
    v = jnp.where(own_entry, -v, v)
    merged = [v[k : k + 1] for k in range(neg)]
    for k in range(neg):
        for j in range(k + 1, neg):
            merged[k] = merged[k] + jnp.where(flat[j : j + 1] == flat[k : k + 1], v[j : j + 1], 0.0)
    v = jnp.concatenate(merged, axis=0)
    shared[0] = jnp.concatenate([v, jnp.broadcast_to(inverse, (8 - neg, rows))], axis=0)

    def sh_copy(i):
        return remote(shared.at[0], shared.at[i], sh_sem, sh_sems.at[i], ahead(i))

    def start_sh(i, carry):
        sh_copy(i).start()
        return carry

    lax.fori_loop(1, n, start_sh, 0)
    for part in range(PARTS):
        start_hop(3, part)
    loss_ref[...] = jnp.log(partition) - positive
    for stop in range(STOPS - 1):
        weight = exps[stop] * inverse
        if stop == 0:
            weight = (weight - jnp.where(eye, 1.0, 0.0)).astype(jnp.bfloat16).astype(jnp.float32)
            p_weight[0] = weight.astype(jnp.bfloat16)
            weight = weight + jnp.where(eye, own_v, 0.0)
        q_weight[stop] = weight.T.astype(jnp.bfloat16)

    def spread(step, carry):
        grads = []
        for part in range(2):
            pos = 2 * step + part

            @pl.when(pos > 0)
            def _():
                sh_copy(pos).wait_recv()

            place = lax.broadcasted_iota(jnp.int32, (places, rows), 0)
            slot = places_of(pos)
            weight = jnp.zeros((places, rows), jnp.float32)
            for k in reversed(range(neg)):
                weight = jnp.where(place == slot[k : k + 1], shared[pos, k : k + 1, :], weight)
            q_side = jnp.maximum(weight, 0.0).astype(jnp.bfloat16)
            p_side = jnp.abs(weight).astype(jnp.bfloat16)
            q_part[pos] = dot(q_side, table[pos], TN)
            grads.append((dot(p_side, w[pos]) / TEMP).reshape(n, SLOTS, 128))
        both = jnp.concatenate(grads, axis=1).astype(jnp.bfloat16)
        sums[:, pl.ds(pl.multiple_of(step * 16, 16), 16), :] = both
        return carry

    lax.fori_loop(0, n // 2, spread, 0)

    def y_copy(pos):
        return remote(y_send.at[pos], y_recv.at[n - pos], y_sem, y_got, behind(pos))

    def gather_tile(pos):
        asked = asks_t[pl.ds(behind(pos), 1), :]
        target = lax.broadcasted_iota(jnp.int32, (rows, places), 0).astype(jnp.float32)
        hot = jnp.where(target == asked, 1.0, 0.0).astype(jnp.bfloat16)
        p_grad = dot(hot, sums[pos])
        lane = lax.broadcasted_iota(jnp.int32, p_grad.shape, 1)
        return jnp.where(lane < 64, p_grad, q_part[pos] / TEMP).astype(jnp.bfloat16)

    def gather_step(pos, carry):
        y_send[pos] = gather_tile(pos)
        y_copy(pos).start()
        return carry

    lax.fori_loop(1, n, gather_step, 0)
    y_recv[0] = gather_tile(0)

    for part in range(PARTS):
        end_hop(3, part)

    def inverse_of(stop):
        return shared[position(lax.rem(me + stop, n)), neg : neg + 1, :]

    for stop in range(1, STOPS):
        p_weight[stop] = (jnp.exp(window_scores(0, stop)) * inverse_of(stop)).astype(jnp.bfloat16)
    q_weight[STOPS - 1] = (jnp.exp(window_scores(STOPS - 1, 0)) * inverse).T.astype(jnp.bfloat16)

    def products(tile, carry):
        cut = pl.ds(pl.multiple_of(tile * 256, 256), 256)
        q_grad = jnp.zeros((rows, 256), jnp.float32)
        p_grad = jnp.zeros((rows, 256), jnp.float32)
        for stop in range(STOPS):
            q_grad = q_grad + dot(q_weight[stop], p_win[stop, :, cut])
            p_grad = p_grad + dot(p_weight[stop], q_win[stop, :, cut])
        q_acc[:, cut] = q_grad / TEMP
        p_acc[:, cut] = p_grad / TEMP
        return carry

    lax.fori_loop(0, width // 256, products, 0)

    all_others(y_recv, y_sem, y_got).wait_recv()

    def finish(chunk, total):
        cut = pl.ds(pl.multiple_of(chunk * 16, 16), 16)
        low = lax.broadcasted_iota(jnp.int32, (16, 128), 1) < 64
        for tile in range(tiles):
            lanes = slice(tile * 128, (tile + 1) * 128)
            even = y_recv[position(2 * tile), cut, :].astype(jnp.float32)
            odd = y_recv[position(2 * tile + 1), cut, :].astype(jnp.float32)
            p_acc[cut, lanes] += jnp.where(low, even, pltpu.roll(odd, 64, 1))
            q_acc[cut, lanes] += jnp.where(low, pltpu.roll(even, 64, 1), odd)
        for src, norm, out in ((q_ref, q_norm, q_acc), (p_ref, p_norm, p_acc)):
            hidden = src[cut, :].astype(jnp.float32)
            over = norm[cut, :1]
            gain = gain_ref[...]
            unit = hidden * gain * over
            grad = out[cut, :]
            inner = jnp.sum(unit * grad, axis=-1, keepdims=True)
            scaled = (grad - unit * inner) * over
            out[cut, :] = scaled * gain
            each = hidden * scaled
            total = total + each[:8] + each[8:]
        return total

    total = lax.fori_loop(0, rows // 16, finish, jnp.zeros((8, width), jnp.float32))

    total = jnp.sum(total, axis=0, keepdims=True)
    each = max(1, tiles // LINE)
    gain_part[...] = jnp.zeros_like(gain_part)
    for tile in range(tiles):
        gain_part[tile // each, tile % each : tile % each + 1, :] = total[:, tile * 128 : (tile + 1) * 128]
    outputs = (pltpu.make_async_copy(q_acc, q_out, out_sems.at[0]), pltpu.make_async_copy(p_acc, p_out, out_sems.at[1]))

    def near_copy(off):
        to = lax.rem(z + off, LINE)
        return remote(gain_part.at[to], gain_near.at[off], g_sems.at[0], g_got.at[0], row * LINE + to)

    size = lines * reps
    spot = row * reps + rep

    def far_copy(off):
        to = lax.rem(spot + off, size)
        return remote(
            gain_far.at[0], gain_far.at[off], g_sems.at[1], g_got.at[1], to // reps * LINE + z, lax.rem(to, reps)
        )

    def all_copy(off):
        to = lax.rem(z + off, LINE)
        return remote(gain_all.at[0], gain_all.at[off], g_sems.at[2], g_got.at[2], row * LINE + to)

    def whole(buffer, turn):
        cut = pl.ds(1, buffer.shape[0] - 1)
        return remote(buffer.at[cut], buffer.at[cut], g_sems.at[turn], g_got.at[turn], right)

    for off in range(1, LINE):
        near_copy(off).start()
    for copy in outputs:
        copy.start()
    whole(gain_near, 0).wait_recv()
    piece = gain_part[z]
    for off in range(1, LINE):
        piece = piece + gain_near[off]
    gain_far[0] = piece

    def start_far(off, carry):
        far_copy(off).start()
        return carry

    lax.fori_loop(1, size, start_far, 0)
    whole(gain_far, 1).wait_recv()
    gain_all[0] = lax.fori_loop(
        0, size, lambda i, add: add + gain_far[lax.rem(spot + size - i, size)], jnp.zeros((8, 128), jnp.float32)
    )
    for off in range(1, LINE):
        all_copy(off).start()
    whole(gain_all, 2).wait_recv()
    for tile in range(tiles):
        gain_out[tile : tile + 1, :] = gain_all[lax.rem(z + LINE - tile // each, LINE), tile % each : tile % each + 1, :]

    all_others(idx_all, idx_sem, idx_got).wait_send()
    all_others(x_send, x_sem, idx_got).wait_send()
    all_others(t_send, t_sem, t_got).wait_send()
    all_others(shared, sh_sem, idx_got).wait_send()
    all_others(y_send, y_sem, y_got).wait_send()
    side.wait_send()
    for turn in range(1, STOPS):
        for part in range(PARTS):
            for copy in hop(turn, part):
                copy.wait_send()
    for turn, buffer in enumerate((gain_near, gain_far, gain_all)):
        whole(buffer, turn).wait_send()
    for copy in outputs:
        copy.wait()


def run(q_hidden, p_hidden, gain, idx):
    n, reps = lax.axis_size("batch"), lax.axis_size("rep")
    rows, width = q_hidden.shape
    half = rows // 2
    places = n * SLOTS
    vmem, hbm = pl.BlockSpec(memory_space=pltpu.VMEM), pl.BlockSpec(memory_space=pl.ANY)
    bf16, f32 = jnp.bfloat16, jnp.float32
    dma = pltpu.SemaphoreType.DMA
    return pl.pallas_call(
        functools.partial(kernel, n, reps),
        in_specs=[hbm, hbm, vmem, vmem],
        out_specs=[hbm, hbm, vmem, vmem],
        out_shape=[
            jax.ShapeDtypeStruct((rows, width), f32),
            jax.ShapeDtypeStruct((rows, width), f32),
            jax.ShapeDtypeStruct((1, rows), f32),
            jax.ShapeDtypeStruct((width // 128, 128), f32),
        ],
        scratch_shapes=[
            pltpu.VMEM((rows, width), bf16),
            pltpu.VMEM((rows, width), bf16),
            pltpu.VMEM((rows, width), f32),
            pltpu.VMEM((rows, width), f32),
            pltpu.VMEM((STOPS, rows, width), bf16),
            pltpu.VMEM((STOPS, rows, width), bf16),
            pltpu.VMEM((n, rows, 128), bf16),
            pltpu.VMEM((n, rows, 128), bf16),
            pltpu.VMEM((n, rows, 128), bf16),
            pltpu.VMEM((n, rows, 128), bf16),
            pltpu.VMEM((n, places, 128), bf16),
            pltpu.VMEM((n, places, 128), bf16),
            pltpu.VMEM((n, rows, 128), f32),
            pltpu.VMEM((n, 2 * SLOTS, 128), bf16),
            pltpu.VMEM((places, 128), bf16),
            pltpu.VMEM((128, places), f32),
            pltpu.VMEM((n, 8, rows), f32),
            pltpu.VMEM((n, 8, rows), f32),
            pltpu.VMEM((n, 8, rows), f32),
            pltpu.VMEM((8, rows), f32),
            pltpu.VMEM((8, rows), f32),
            pltpu.VMEM((rows, 128), f32),
            pltpu.VMEM((rows, 128), f32),
            pltpu.VMEM((STOPS, rows, rows), bf16),
            pltpu.VMEM((STOPS, rows, rows), bf16),
            pltpu.VMEM((LINE, 8, 128), f32),
            pltpu.VMEM((LINE, 8, 128), f32),
            pltpu.VMEM((n // LINE * reps, 8, 128), f32),
            pltpu.VMEM((LINE, 8, 128), f32),
            dma((2,)),
            dma((2,)),
            dma,
            dma((n,)),
            dma,
            dma,
            dma,
            dma,
            dma,
            dma((n,)),
            dma,
            dma,
            dma((2, STOPS - 1, PARTS)),
            dma((2, STOPS - 1, PARTS)),
            dma,
            dma,
            dma((3,)),
            dma((3,)),
        ],
        compiler_params=pltpu.CompilerParams(
            collective_id=0, has_side_effects=True, vmem_limit_bytes=60 * MIB
        ),
        name="contrastive",
    )(q_hidden, p_hidden, gain.reshape(1, width), idx)


def local(query_hidden, passage_hidden, norm_gain, negatives):
    query_grad, passage_grad, loss, gain_grad = run(query_hidden[0], passage_hidden[0], norm_gain, negatives[0].T)
    return (query_grad[None], passage_grad[None], loss, gain_grad.reshape(norm_gain.shape))


def solution(mesh):
    return jax.shard_map(
        local,
        mesh=mesh,
        in_specs=(P("rep", "batch", None), P("rep", "batch", None), P(), P("rep", "batch", None)),
        out_specs=(P("rep", "batch", None), P("rep", "batch", None), P("rep", "batch"), P()),
        check_vma=False,
    )
```
